32 devices in a mesh: ctx: 8 (over y, x, core), inner: 4 (over z).
Axes of the slice: x: 2, y: 2, z: 4, core: 2. Of those that a mesh axis runs over, the one named last changes fastest.
Arguments:
- low_rank: bfloat16 [2048, 32], P(('ctx', 'inner')), may hold values from -6 to 6
- q_base: bfloat16 [2048, 4608], P(('ctx', 'inner')), may hold values from -6 to 6
- k_base: bfloat16 [2048, 4608], P(('ctx', 'inner')), may hold values from -6 to 6
- v_base: bfloat16 [2048, 4608], P(('ctx', 'inner')), may hold values from -6 to 6
- edit_up: bfloat16 [32, 13824], replicated, may hold values from -0.5 to 0.5
- log_decay: bfloat16 [2048, 36], P(('ctx', 'inner')), may hold values from -1 to 0
- lengths: int32 [8], P('ctx'), may hold values from 128 to 256, as said below
- norm_gain: float32 [4608], replicated, may hold values from 0.5 to 1.5
Outputs:
- attended: bfloat16 [2048, 4608], P(('ctx', 'inner'))
The draws below stay inside these ranges and needn't reach their ends.
Inputs may be any that keep to these rules, and one draw needn't show every extreme that they name: `lengths`: every segment keeps at least half of its tokens, and some segment is full.
All inputs are finite; a program needn't handle non-finite values.
Results may differ from the reference program's by a relative error of at most 0.0072.
Values may be sent and summed in bfloat16 or wider, within the bound.
No kernel may reach another device: no remote copies, remote signals or barrier semaphores. Data moves between devices by JAX's collectives and lax.ppermute only.
A program may use at most 64 MiB of HBM per device.

```python
import math
import jax
import jax.numpy as jnp
from jax import lax

DECAYING_HEADS = 36
DH = 128
R = 32
SEG_TOK = 256
SEGS = 8
DOCUMENT_TOKENS = 2048
HD = 4608
N_INNER = 4


def segment_gain(key):
    gain_key = jax.random.fold_in(key, 7001)
    phase_key, loud_key, quiet_key = jax.random.split(gain_key, 3)
    loud_span = max(2, min(16, SEGS // 4))
    start_phase = jax.random.randint(phase_key, (), 0, loud_span)
    segment_ids = jnp.arange(SEGS, dtype=jnp.int32)
    loud_flag = ((segment_ids + start_phase) % loud_span == 0) | (segment_ids == SEGS // 2)
    loud_gain = jnp.exp(jax.random.uniform(loud_key, (SEGS,), jnp.float32, jnp.log(0.5), jnp.log(1.0)))
    quiet_gain = jnp.exp(jax.random.uniform(quiet_key, (SEGS,), jnp.float32, jnp.log(0.004), jnp.log(0.012)))
    return jnp.repeat(jnp.where(loud_flag, loud_gain, quiet_gain), SEG_TOK)


def gained_field(key, salt_value, columns):
    field_key = jax.random.fold_in(key, salt_value)
    noise_field = jax.random.truncated_normal(field_key, -6.0, 6.0, (DOCUMENT_TOKENS, columns), jnp.float32)
    return (noise_field * segment_gain(key)[:, None]).astype(jnp.bfloat16)


def draw_low_rank(key, part):
    return gained_field(key, 11, R)


def draw_k_base(key, part):
    return gained_field(key, 12, HD)


def draw_v_base(key, part):
    return gained_field(key, 13, HD)


def draw_log_decay(key, part):
    gathered_keys = jax.random.split(key, 9)
    fast_count = max(1, DECAYING_HEADS // 2)
    slow_low = 0.6
    slow_high = 1.8
    head_order = jax.random.permutation(gathered_keys[0], DECAYING_HEADS)
    rapid_decay_heads = head_order < fast_count
    slow_rate = jnp.exp(jax.random.uniform(gathered_keys[1], (DECAYING_HEADS,), jnp.float32, jnp.log(slow_low), jnp.log(slow_high))) / SEG_TOK
    fast_base = jnp.exp(jax.random.uniform(gathered_keys[2], (DECAYING_HEADS,), jnp.float32, jnp.log(0.1), jnp.log(0.3))) / SEG_TOK
    per_head_decay = jnp.where(rapid_decay_heads, fast_base, slow_rate)
    segment_multiplier = jnp.exp(jax.random.uniform(gathered_keys[3], (SEGS, 1, DECAYING_HEADS), jnp.float32, jnp.log(0.5), jnp.log(2.0)))
    segment_multiplier = jnp.broadcast_to(segment_multiplier, (SEGS, SEG_TOK, DECAYING_HEADS)).reshape(DOCUMENT_TOKENS, DECAYING_HEADS)
    random_offset = jnp.exp(jax.random.uniform(gathered_keys[4], (DOCUMENT_TOKENS, DECAYING_HEADS), jnp.float32, jnp.log(0.5), jnp.log(2.0)))
    gentle_component = -per_head_decay[None, :] * segment_multiplier * random_offset
    sudden_rows = jax.random.uniform(gathered_keys[5], (DOCUMENT_TOKENS, DECAYING_HEADS), jnp.float32) < 1.0 / 40.0
    sudden_magnitude = jax.random.uniform(gathered_keys[6], (DOCUMENT_TOKENS, DECAYING_HEADS), jnp.float32, 0.6, 0.95)
    sudden_component = jnp.where(sudden_rows & rapid_decay_heads[None, :], -sudden_magnitude, 0.0)
    spike_position = jax.random.randint(gathered_keys[7], (3,), 0, DOCUMENT_TOKENS)
    outlier_rows = jnp.any(jnp.arange(DOCUMENT_TOKENS)[:, None] == spike_position[None, :], axis=1)
    outlier_weight = jnp.log(jax.random.uniform(gathered_keys[8], (DOCUMENT_TOKENS, DECAYING_HEADS), jnp.float32, 0.55, 0.8))
    merged_output = gentle_component + sudden_component + jnp.where(outlier_rows[:, None], outlier_weight, 0.0)
    return jnp.clip(merged_output, -1.0, 0.0).astype(jnp.bfloat16)


def draw_lengths(key, part):
    first_key, second_key = jax.random.split(key, 2)
    drawn = jax.random.randint(first_key, (SEGS,), SEG_TOK // 2, SEG_TOK + 1)
    full_one = jax.random.randint(second_key, (), 0, SEGS)
    return jnp.where(jnp.arange(SEGS) == full_one, SEG_TOK, drawn).astype(jnp.int32)


def level_of(rng, dims, cuts, low, largest):
    def one(position, blocks):
        draws = jax.random.uniform(jax.random.fold_in(jax.random.fold_in(rng, 6), position), (blocks,), jnp.float32, low / len(cuts), largest / len(cuts))
        return jnp.repeat(jnp.exp(draws), dims[position] // blocks).reshape((-1,) + (1,) * (len(dims) - position - 1))

    loudness = one(*cuts[0])
    for cut in cuts[1:]:
        loudness = loudness * one(*cut)
    return loudness


def gaussian(rng, dims, spread, limit, cuts=(), kind=jnp.bfloat16):
    values = spread * jax.random.normal(rng, dims, jnp.float32)
    if cuts:
        values = values * level_of(rng, dims, cuts, -0.22, 0.18)
    return jnp.clip(values, -limit, limit).astype(kind)


def setup_inputs(seed: int = 0) -> dict:
    key_list = jax.random.split(jax.random.key(seed), 9)
    low_rank = draw_low_rank(jax.random.fold_in(key_list[8], 71), 0)
    q_base = gaussian(key_list[1], (DOCUMENT_TOKENS, HD), 1.0, 6.0, ((0, 32),))
    k_base = draw_k_base(jax.random.fold_in(key_list[8], 71), 0)
    v_base = draw_v_base(jax.random.fold_in(key_list[8], 71), 0)
    edit_up = gaussian(key_list[4], (R, 3 * HD), (4 * R) ** -0.5, 0.5)
    log_decay = draw_log_decay(jax.random.fold_in(key_list[8], 71), 0)
    lengths = draw_lengths(jax.random.fold_in(key_list[8], 71), 0)
    norm_gain = jnp.clip(1.0 + 0.1 * jax.random.normal(key_list[7], (HD,), jnp.float32), 0.5, 1.5)
    return dict(low_rank=low_rank, q_base=q_base, k_base=k_base, v_base=v_base, edit_up=edit_up, log_decay=log_decay, lengths=lengths, norm_gain=norm_gain)


def rounded(values):
    return lax.optimization_barrier(values.astype(jnp.bfloat16)).astype(jnp.float32)

def reference(low_rank, q_base, k_base, v_base, edit_up, log_decay, lengths, norm_gain):
    full_width = DECAYING_HEADS * DH
    tile_count = math.gcd(N_INNER, max(1, SEG_TOK // 512))
    block_rows = SEG_TOK // tile_count
    order_ids = jnp.arange(block_rows, dtype=jnp.int32)
    causal = (order_ids[:, None] >= order_ids[None, :])[None]

    def segment(carry_state, inputs):
        rank_rows, q_rows, k_rows, v_rows, decay_rows, seg_length = inputs
        edit_term = jnp.dot(rank_rows, edit_up, preferred_element_type=jnp.float32)
        positions = jnp.arange(SEG_TOK, dtype=jnp.int32)
        live_rows = (positions < seg_length)[:, None]
        queries = rounded(q_rows.astype(jnp.float32) + edit_term[:, :full_width])
        keys_all = rounded(jnp.where(live_rows, k_rows.astype(jnp.float32) + edit_term[:, full_width:2 * full_width], 0.0))
        values_all = rounded(jnp.where(live_rows, v_rows.astype(jnp.float32) + edit_term[:, 2 * full_width:], 0.0))
        query_heads = queries.reshape(SEG_TOK, DECAYING_HEADS, DH)
        key_heads = keys_all.reshape(SEG_TOK, DECAYING_HEADS, DH)
        value_heads = values_all.reshape(SEG_TOK, DECAYING_HEADS, DH)
        decay_sum = jnp.cumsum(decay_rows.astype(jnp.float32), axis=0)
        ending = decay_sum[-1]
        scaled = rounded(key_heads * jnp.exp(ending[None, :] - decay_sum)[:, :, None])
        seg_state = jnp.einsum('shd,she->hde', scaled, value_heads)
        sum_heads = decay_sum.T
        pieces = []
        for first in range(tile_count):
            lower = first * block_rows
            query_part = query_heads[lower:lower + block_rows]
            total = jnp.zeros((block_rows, DECAYING_HEADS, DH), jnp.float32)
            for second in range(first + 1):
                start = second * block_rows
                key_part = key_heads[start:start + block_rows]
                value_part = value_heads[start:start + block_rows]
                scores = jnp.einsum('thd,shd->hts', query_part, key_part)
                gap_log = sum_heads[:, lower:lower + block_rows, None] - sum_heads[:, None, start:start + block_rows]
                if second == first:
                    weights = rounded(jnp.where(causal, scores * jnp.exp(jnp.where(causal, gap_log, 0.0)), 0.0))
                else:
                    weights = rounded(scores * jnp.exp(gap_log))
                total = total + jnp.einsum('hts,shd->thd', weights, value_part)
            pieces.append(total)
        intra_term = jnp.concatenate(pieces, axis=0)
        former = rounded(carry_state)
        inter_term = jnp.exp(decay_sum)[:, :, None] * jnp.einsum('thd,hde->the', query_heads, former)
        mixed_out = (intra_term + inter_term).astype(jnp.bfloat16).reshape(SEG_TOK, full_width)
        mixed_out = jnp.where(live_rows, mixed_out, jnp.zeros_like(mixed_out))
        flat_out = mixed_out.astype(jnp.float32)
        inv_rms = lax.rsqrt(lax.optimization_barrier(jnp.mean(flat_out * flat_out, axis=-1, keepdims=True)) + 1e-06)
        attended = (flat_out * inv_rms * norm_gain[None, :]).astype(jnp.bfloat16)
        next_state = jnp.exp(ending)[:, None, None] * carry_state + seg_state
        return (next_state, attended)
    start_state = jnp.zeros((DECAYING_HEADS, DH, DH), jnp.float32)
    inputs = (low_rank.reshape(SEGS, SEG_TOK, R), q_base.reshape(SEGS, SEG_TOK, full_width), k_base.reshape(SEGS, SEG_TOK, full_width), v_base.reshape(SEGS, SEG_TOK, full_width), log_decay.reshape(SEGS, SEG_TOK, DECAYING_HEADS), lengths.astype(jnp.int32))
    final_state, outputs = lax.scan(segment, start_state, inputs)
    return outputs.reshape(DOCUMENT_TOKENS, full_width)
```

```python
import jax
import jax.numpy as jnp
from jax import lax
from jax.experimental import pallas as pl
from jax.experimental.pallas import tpu as pltpu
from jax.sharding import PartitionSpec as P

F32, BF16 = jnp.float32, jnp.bfloat16
LANES = 128
PAD = 16
PARTS = 2
PARAMS = pltpu.CompilerParams(vmem_limit_bytes=48 * 1024 * 1024)
SMEM = pl.BlockSpec(memory_space=pltpu.SMEM)


def dot(a, b, dims):
    return lax.dot_general(a, b, ((dims[:1], dims[1:]), ((), ())), preferred_element_type=F32)


def call(kernel, shapes, args, specs=None, scratch=()):
    whole = [pl.BlockSpec(memory_space=pltpu.VMEM)] * len(args) if specs is None else specs
    return pl.pallas_call(
        kernel,
        grid=(1,),
        out_shape=[jax.ShapeDtypeStruct(*shape) for shape in shapes],
        in_specs=whole,
        out_specs=[pl.BlockSpec(memory_space=pltpu.VMEM)] * len(shapes),
        scratch_shapes=list(scratch),
        compiler_params=PARAMS,
    )(*args)


def live_mask(len_ref, rows):
    at = lax.axis_index("inner") * rows + lax.broadcasted_iota(jnp.int32, (rows, 1), 0)
    return at < len_ref[0]


class Sizes:
    def __init__(self, q_base, log_decay):
        self.n = lax.axis_size("inner")
        self.rows, self.width = q_base.shape
        self.heads = log_decay.shape[1]
        self.local = self.heads // self.n
        self.dh = self.width // self.heads
        self.seg = self.rows * self.n
        self.steps = (lax.axis_size("ctx") - 1).bit_length()
        first = -(-self.local // PARTS)
        self.parts = []
        at = 0
        while at < self.local:
            self.parts.append((at, min(first, self.local - at)))
            at += first


def project(z, names, part, lengths, low_rank, bases, edit_up, columns, log_decay=None):
    h0, count = part
    n, rows, dh = z.n, z.rows, z.dh
    kinds = len(bases)
    height = kinds * count * rows + (PAD if log_decay is not None else 0)

    def kernel(len_ref, lr_ref, *refs):
        base_refs, up_refs = refs[:kinds], refs[kinds : 2 * kinds]
        ld_ref = refs[2 * kinds] if log_decay is not None else None
        outs = refs[-n:]
        me = lax.axis_index("inner")
        live = live_mask(len_ref, rows)
        low = lr_ref[...]
        for k in range(n):
            group = lax.rem(me + k, n)
            at = pl.multiple_of((group * z.local + h0) * dh, LANES)
            cols = pl.ds(at, count * dh)
            for kind in range(kinds):
                term = dot(low, up_refs[kind][:, cols], (1, 0))
                edited = base_refs[kind][:, cols].astype(F32) + term
                if names[kind] != "q":
                    edited = jnp.where(live, edited, 0.0)
                edited = edited.astype(BF16)
                for h in range(count):
                    top = (kind * count + h) * rows
                    outs[k][top : top + rows, :] = edited[:, h * dh : (h + 1) * dh]
            if ld_ref is not None:
                row = lax.broadcasted_iota(jnp.int32, (PAD, z.heads), 0)
                col = lax.broadcasted_iota(jnp.int32, (PAD, z.heads), 1)
                pick = jnp.where((row < z.local) & (col == row + group * z.local), 1.0, 0.0).astype(BF16)
                wide = jnp.concatenate(
                    [dot(pick, ld_ref[...], (1, 1)), jnp.zeros((PAD, LANES - rows), F32)], axis=1
                )
                outs[k][height - PAD : height, :] = wide.astype(BF16)

    vm = pl.BlockSpec(memory_space=pltpu.VMEM)
    args = [lengths, low_rank, *bases, *([edit_up] * kinds)]
    specs = [SMEM, vm, *([vm] * kinds)]
    specs += [pl.BlockSpec((edit_up.shape[0], z.width), lambda _, c=c: (0, c)) for c in columns]
    if log_decay is not None:
        args.append(log_decay)
        specs.append(vm)
    return call(kernel, [((height, dh), BF16)] * n, args, specs)


def scatter_heads(z, refs, held, first, count):
    me = lax.axis_index("inner")
    for k in range(z.n):
        chunk = lax.rem(me + (z.n - k), z.n)
        at = pl.ds(pl.multiple_of(chunk * z.rows, z.rows), z.rows)
        for h in range(count):
            top = (first + h) * z.rows
            held[h, at, :] = refs[k][top : top + z.rows, :]


def segment_states(z, part, blocks, decays=None):
    h0, count = part
    n, rows, dh, seg = z.n, z.rows, z.dh, z.seg
    first = decays is None

    def kernel(*refs):
        kv = refs[:n]
        if first:
            state, send, col_ref, row_ref, ks, vs, lds = refs[n:]
        else:
            col_ref, row_ref, state, send, ks, vs = refs[n:]
        scatter_heads(z, kv, ks, 0, count)
        scatter_heads(z, kv, vs, count, count)
        if first:
            me = lax.axis_index("inner")
            for k in range(n):
                lds[lax.rem(me + (n - k), n)] = kv[k][2 * count * rows :, :]
            t = lax.broadcasted_iota(jnp.int32, (rows, LANES), 0)
            s = lax.broadcasted_iota(jnp.int32, (rows, LANES), 1)
            tri = jnp.where(s <= t, 1.0, 0.0).astype(BF16)
            so_far = jnp.zeros((1, PAD), F32)
            for j in range(n):
                cum = dot(tri, lds[j], (1, 1)) + so_far
                so_far = cum[rows - 1 : rows, :]
                wide = jnp.concatenate([cum, jnp.zeros((rows, LANES - PAD), F32)], axis=1)
                col_ref[j * rows : (j + 1) * rows, :] = wide
            row_ref[...] = col_ref[...].T[:PAD, :]
        col = col_ref[...]
        scale = jnp.exp(col[seg - 1 : seg, :] - col)
        for h in range(count):
            scaled = (ks[h].astype(F32) * scale[:, h0 + h : h0 + h + 1]).astype(BF16)
            value = dot(scaled, vs[h], (0, 0))
            state[h * dh : (h + 1) * dh, :] = value
            send[h * dh : (h + 1) * dh, :] = value.astype(BF16)
        put_sums(send, count * dh, jnp.broadcast_to(row_ref[:, seg - 1 : seg], (PAD, LANES)))

    shapes = [((count * dh, dh), F32), ((count * dh + 2 * PAD, dh), BF16)]
    scratch = [pltpu.VMEM((count, seg, dh), BF16)] * 2
    if first:
        shapes += [((seg, LANES), F32), ((PAD, seg), F32)]
        scratch.append(pltpu.VMEM((n, PAD, LANES), BF16))
    return call(kernel, shapes, [*blocks, *(decays or ())], scratch=scratch)


def put_sums(send, at, sums):
    high = sums.astype(BF16)
    send[at : at + PAD, :] = high
    send[at + PAD : at + 2 * PAD, :] = (sums - high.astype(F32)).astype(BF16)


def get_sums(got, at):
    return got[at : at + PAD, :].astype(F32) + got[at + PAD : at + 2 * PAD, :].astype(F32)


def is_later(step):
    return lax.rem(lax.axis_index("ctx") // (1 << step), 2) == 1


def join(z, step, part, total, got, sums, carried=None):
    h0, count = part
    dh = z.dh

    def kernel(*refs):
        total_ref, got_ref, sums_ref = refs[:3]
        carried_ref = refs[3] if carried is not None else None
        new_total, new_carried, send, new_sums = refs[-4:]
        later = is_later(step)
        own = sums_ref[...] if carried is None else sums_ref[:PAD, :]
        if carried is None:
            own = jnp.broadcast_to(own[:, z.seg - 1 : z.seg], (PAD, LANES))
            before = jnp.zeros((PAD, LANES), F32)
        else:
            before = sums_ref[PAD:, :]
        other = get_sums(got_ref, count * dh)
        keep = jnp.where(later, 1.0, jnp.exp(other))
        take = jnp.where(later, jnp.exp(own), 1.0)
        carry = jnp.where(later, jnp.exp(before), 0.0)
        for h in range(count):
            at = slice(h * dh, (h + 1) * dh)
            row = slice(h0 + h, h0 + h + 1)
            theirs = got_ref[at, :].astype(F32)
            value = total_ref[at, :] * keep[row, :] + theirs * take[row, :]
            new_total[at, :] = value
            send[at, :] = value.astype(BF16)
            moved = theirs * carry[row, :]
            new_carried[at, :] = moved if carried is None else carried_ref[at, :] + moved
        put_sums(send, count * dh, own + other)
        new_sums[:PAD, :] = own + other
        new_sums[PAD:, :] = before + jnp.where(later, other, 0.0)

    shapes = [((count * dh, dh), F32)] * 2 + [((count * dh + 2 * PAD, dh), BF16), ((2 * PAD, LANES), F32)]
    args = [total, got, sums] + ([] if carried is None else [carried])
    return call(kernel, shapes, args)


def attend(z, part, kv, qs_in, col, row, carried, got, sums):
    h0, count = part
    n, rows, dh, seg = z.n, z.rows, z.dh, z.seg

    def kernel(*refs):
        kv_refs, q_refs = refs[:n], refs[n : 2 * n]
        col_ref, row_ref, carried_ref, got_ref, sums_ref = refs[2 * n : 2 * n + 5]
        outs = refs[2 * n + 5 : 3 * n + 5]
        ks, vs, qs, mixed = refs[3 * n + 5 :]
        scatter_heads(z, kv_refs, ks, 0, count)
        scatter_heads(z, kv_refs, vs, count, count)
        scatter_heads(z, q_refs, qs, 0, count)
        later = is_later(z.steps - 1)
        carry = jnp.where(later, jnp.exp(sums_ref[PAD:, :]), 0.0)
        t = lax.broadcasted_iota(jnp.int32, (seg, seg), 0)
        s = lax.broadcasted_iota(jnp.int32, (seg, seg), 1)
        causal = s <= t
        for h in range(count):
            at = slice(h * dh, (h + 1) * dh)
            former = carried_ref[at, :] + got_ref[at, :].astype(F32) * carry[h0 + h : h0 + h + 1, :]
            q = qs[h]
            d_col = col_ref[:, h0 + h : h0 + h + 1]
            scores = dot(q, ks[h], (1, 1))
            gap = jnp.where(causal, d_col - row_ref[h0 + h : h0 + h + 1, :], 0.0)
            weights = jnp.where(causal, scores * jnp.exp(gap), 0.0).astype(BF16)
            out = dot(weights, vs[h], (1, 0)) + jnp.exp(d_col) * dot(q, former.astype(BF16), (1, 0))
            mixed[:, at] = out.astype(BF16)
        me = lax.axis_index("inner")
        for k in range(n):
            chunk = lax.rem(me + k, n)
            outs[k][...] = mixed[pl.ds(pl.multiple_of(chunk * rows, rows), rows), :]

    scratch = [pltpu.VMEM((count, seg, dh), BF16)] * 3 + [pltpu.VMEM((seg, count * dh), BF16)]
    args = [*kv, *qs_in, col, row, carried, got, sums]
    return call(kernel, [((rows, count * dh), BF16)] * n, args, scratch=scratch)


def normalize(z, lengths, gain, blocks):
    n, rows, dh = z.n, z.rows, z.dh

    def kernel(len_ref, gain_ref, *refs):
        out = refs[-1]
        me = lax.axis_index("inner")
        live = live_mask(len_ref, rows)
        total = jnp.zeros((rows, 1), F32)
        for ref in refs[:-1]:
            flat = ref[...].astype(F32)
            total = total + jnp.sum(flat * flat, axis=1, keepdims=True)
        inv = lax.rsqrt(total / z.width + 1e-06)
        for p, (h0, count) in enumerate(z.parts):
            for k in range(n):
                group = lax.rem(me + (n - k), n)
                cols = pl.ds(pl.multiple_of((group * z.local + h0) * dh, LANES), count * dh)
                scaled = refs[p * n + k][...].astype(F32) * inv * gain_ref[:, cols]
                out[:, cols] = jnp.where(live, scaled, 0.0).astype(BF16)

    flat_blocks = [block for part in blocks for block in part]
    args = [lengths, gain, *flat_blocks]
    specs = [SMEM] + [pl.BlockSpec(memory_space=pltpu.VMEM)] * (len(args) - 1)
    return call(kernel, [((rows, z.width), BF16)], args, specs)[0]


def shift_blocks(z, blocks):
    n = z.n
    return [blocks[0]] + [
        lax.ppermute(blocks[k], "inner", [(i, (i + k) % n) for i in range(n)]) for k in range(1, n)
    ]


def shards(low_rank, q_base, k_base, v_base, edit_up, log_decay, lengths, norm_gain):
    z = Sizes(q_base, log_decay)
    ctx = lax.axis_size("ctx")
    kv, qs, outs = [], [], []
    for p, part in enumerate(z.parts):
        blocks = project(
            z, "kv", part, lengths, low_rank, (k_base, v_base), edit_up, (1, 2), log_decay if p == 0 else None
        )
        kv.append(shift_blocks(z, blocks))
    for part in z.parts:
        qs.append(shift_blocks(z, project(z, "q", part, lengths, low_rank, (q_base,), edit_up, (0,))))
    decays = None
    for p, part in enumerate(z.parts):
        total, send, *made = segment_states(z, part, kv[p], decays)
        decays = decays or made
        carried, sums = None, decays[1]
        for step in range(z.steps):
            hop = 1 << step
            last = step == z.steps - 1
            pairs = [(i, i ^ hop) for i in range(ctx) if not (last and i & hop)]
            got = lax.ppermute(send, "ctx", pairs)
            if not last:
                total, carried, send, sums = join(z, step, part, total, got, sums, carried)
        outs.append(shift_blocks(z, attend(z, part, kv[p], qs[p], *decays, carried, got, sums)))
    return normalize(z, lengths, norm_gain[None, :], outs)


def solution(mesh):
    rows = P(("ctx", "inner"), None)
    return jax.shard_map(
        shards,
        mesh=mesh,
        in_specs=(rows, rows, rows, rows, P(), rows, P("ctx"), P()),
        out_specs=rows,
        check_vma=False,
    )
```

```python
import jax
import jax.numpy as jnp
from jax import lax
from jax.experimental import pallas as pl
from jax.experimental.pallas import tpu as pltpu
from jax.sharding import PartitionSpec as P

F32, BF16 = jnp.float32, jnp.bfloat16
LANES = 128
PAD = 16
PARTS = 2
PARAMS = pltpu.CompilerParams(vmem_limit_bytes=48 * 1024 * 1024)
COST = pl.CostEstimate(flops=1_000_000_000, bytes_accessed=1, transcendentals=0)
SMEM = pl.BlockSpec(memory_space=pltpu.SMEM)


def dot(a, b, dims):
    return lax.dot_general(a, b, ((dims[:1], dims[1:]), ((), ())), preferred_element_type=F32)


def call(kernel, shapes, args, specs=None, scratch=(), after=()):
    whole = [pl.BlockSpec(memory_space=pltpu.VMEM)] * len(args) if specs is None else specs
    if after:
        inner, used = kernel, len(args)

        def kernel(*refs):
            inner(*refs[:used], *refs[used + len(after) :])

        args = [*args, *after]
        whole = [*whole, *([pl.BlockSpec(memory_space=pl.ANY)] * len(after))]
    return pl.pallas_call(
        kernel,
        out_shape=[jax.ShapeDtypeStruct(*shape) for shape in shapes],
        in_specs=whole,
        out_specs=[pl.BlockSpec(memory_space=pltpu.VMEM)] * len(shapes),
        scratch_shapes=list(scratch),
        compiler_params=PARAMS,
        cost_estimate=COST,
    )(*args)


def gate(arrays, after):
    every = pl.BlockSpec(memory_space=pl.ANY)
    return pl.pallas_call(
        lambda *refs: None,
        out_shape=[jax.ShapeDtypeStruct(a.shape, a.dtype) for a in arrays],
        in_specs=[every] * (len(arrays) + len(after)),
        out_specs=[every] * len(arrays),
        input_output_aliases={i: i for i in range(len(arrays))},
        compiler_params=PARAMS,
    )(*arrays, *after)


def live_mask(len_ref, rows):
    at = lax.axis_index("inner") * rows + lax.broadcasted_iota(jnp.int32, (rows, 1), 0)
    return at < len_ref[0]


class Sizes:
    def __init__(self, q_base, log_decay):
        self.n = lax.axis_size("inner")
        self.rows, self.width = q_base.shape
        self.heads = log_decay.shape[1]
        self.local = self.heads // self.n
        self.dh = self.width // self.heads
        self.seg = self.rows * self.n
        bits = (lax.axis_size("ctx") - 1).bit_length()
        self.steps = [(at, 1) for at in range(bits)]
        first = -(-self.local // PARTS)
        self.parts = []
        at = 0
        while at < self.local:
            self.parts.append((at, min(first, self.local - at)))
            at += first


def project(z, names, part, lengths, low_rank, bases, edit_up, columns, log_decay, decays, after=()):
    h0, count = part
    n, rows, dh = z.n, z.rows, z.dh
    kinds = len(bases)
    rank = edit_up.shape[0]
    height = kinds * count * rows + (PAD if decays else 0)

    def kernel(len_ref, lr_ref, *refs):
        base_refs, up_ref, ld_from = refs[:kinds], refs[kinds], refs[kinds + 1]
        outs = refs[-n - 5 : -5]
        base_buf, up_buf, low_buf, ld_ref, sems = refs[-5:]
        me = lax.axis_index("inner")

        def copies(k):
            at = (lax.rem(me + k, n) * z.local + h0) * dh
            for kind in range(kinds):
                cols = pl.ds(pl.multiple_of(at, LANES), count * dh)
                up_cols = pl.ds(pl.multiple_of(at + columns[kind] * z.width, LANES), count * dh)
                slot = k * kinds + kind
                yield pltpu.make_async_copy(base_refs[kind].at[:, cols], base_buf.at[slot], sems.at[0, slot])
                yield pltpu.make_async_copy(up_ref.at[:, up_cols], up_buf.at[slot], sems.at[1, slot])

        small = [
            pltpu.make_async_copy(lr_ref, low_buf, sems.at[0, n * kinds]),
            pltpu.make_async_copy(ld_from, ld_ref, sems.at[1, n * kinds]),
        ]
        order = [*range(1, n), 0]
        for copy in small:
            copy.start()
        for k in order:
            for copy in copies(k):
                copy.start()
        live = live_mask(len_ref, rows)
        for copy in small:
            copy.wait()
        low = low_buf[...].T
        for k in order:
            for copy in copies(k):
                copy.wait()
            for kind in range(kinds):
                slot = k * kinds + kind
                edited = base_buf[slot].astype(F32) + dot(low, up_buf[slot], (1, 0))
                if names[kind] != "q":
                    edited = jnp.where(live, edited, 0.0)
                edited = edited.astype(BF16)
                for h in range(count):
                    top = (kind * count + h) * rows
                    outs[k][top : top + rows, :] = edited[:, h * dh : (h + 1) * dh]
            if decays:
                row = lax.broadcasted_iota(jnp.int32, (PAD, z.heads), 0)
                col = lax.broadcasted_iota(jnp.int32, (PAD, z.heads), 1)
                group = lax.rem(me + k, n)
                pick = jnp.where((row < z.local) & (col == row + group * z.local), 1.0, 0.0).astype(BF16)
                wide = jnp.concatenate(
                    [dot(pick, ld_ref[...], (1, 0)), jnp.zeros((PAD, LANES - rows), F32)], axis=1
                )
                outs[k][height - PAD : height, :] = wide.astype(BF16)

    args = [lengths, *(pltpu.with_memory_space_constraint(a, pltpu.HBM) for a in (low_rank, *bases, edit_up, log_decay))]
    specs = [SMEM, *([pl.BlockSpec(memory_space=pltpu.HBM)] * (kinds + 3))]
    scratch = [
        pltpu.VMEM((n * kinds, rows, count * dh), BF16),
        pltpu.VMEM((n * kinds, rank, count * dh), BF16),
        pltpu.VMEM(low_rank.shape, BF16),
        pltpu.VMEM(log_decay.shape, BF16),
        pltpu.SemaphoreType.DMA((2, n * kinds + 1)),
    ]
    return call(kernel, [((height, dh), BF16)] * n, args, specs, scratch, after)


def scatter_heads(z, refs, held, first, count):
    me = lax.axis_index("inner")
    for k in range(z.n):
        chunk = lax.rem(me + (z.n - k), z.n)
        at = pl.ds(pl.multiple_of(chunk * z.rows, z.rows), z.rows)
        for h in range(count):
            top = (first + h) * z.rows
            held[h, at, :] = refs[k][top : top + z.rows, :]


def segment_states(z, kv):
    n, rows, dh, seg, heads = z.n, z.rows, z.dh, z.seg, z.local

    def kernel(*refs):
        kv_refs = refs[:n]
        col_ref, row_ref = refs[n : n + 2]
        results = refs[n + 2 : n + 2 + 2 * len(z.parts)]
        ks, vs, lds = refs[-3:]
        me = lax.axis_index("inner")
        for k in range(n):
            lds[lax.rem(me + (n - k), n)] = kv_refs[k][2 * heads * rows :, :]
        t = lax.broadcasted_iota(jnp.int32, (rows, LANES), 0)
        s = lax.broadcasted_iota(jnp.int32, (rows, LANES), 1)
        tri = jnp.where(s <= t, 1.0, 0.0).astype(BF16)
        so_far = jnp.zeros((1, PAD), F32)
        for j in range(n):
            cum = dot(tri, lds[j], (1, 1)) + so_far
            so_far = cum[rows - 1 : rows, :]
            wide = jnp.concatenate([cum, jnp.zeros((rows, LANES - PAD), F32)], axis=1)
            col_ref[j * rows : (j + 1) * rows, :] = wide
        row_ref[...] = col_ref[...].T[:PAD, :]
        scatter_heads(z, kv_refs, ks, 0, heads)
        scatter_heads(z, kv_refs, vs, heads, heads)
        col = col_ref[...]
        scale = jnp.exp(col[seg - 1 : seg, :] - col)
        ending = jnp.broadcast_to(row_ref[:, seg - 1 : seg], (PAD, LANES))
        for p, (h0, count) in enumerate(z.parts):
            state, send = results[2 * p : 2 * p + 2]
            for h in range(count):
                scaled = (ks[h0 + h].astype(F32) * scale[:, h0 + h : h0 + h + 1]).astype(BF16)
                value = dot(scaled, vs[h0 + h], (0, 0))
                state[h * dh : (h + 1) * dh, :] = value
                send[h * dh : (h + 1) * dh, :] = value.astype(BF16)
            put_sums(send, count * dh, ending)

    shapes = [((seg, LANES), F32), ((PAD, seg), F32)]
    for _, count in z.parts:
        shapes += [((count * dh, dh), F32), ((count * dh + 2 * PAD, dh), BF16)]
    scratch = [pltpu.VMEM((heads, seg, dh), BF16)] * 2 + [pltpu.VMEM((n, PAD, LANES), BF16)]
    return call(kernel, shapes, kv, scratch=scratch)


def put_sums(send, at, sums):
    high = sums.astype(BF16)
    send[at : at + PAD, :] = high
    send[at + PAD : at + 2 * PAD, :] = (sums - high.astype(F32)).astype(BF16)


def get_sums(got, at):
    return got[at : at + PAD, :].astype(F32) + got[at + PAD : at + 2 * PAD, :].astype(F32)


def digit_of(step):
    shift, width = step
    return lax.rem(lax.axis_index("ctx") // (1 << shift), 1 << width)


def exchange(step, last, send):
    shift, width = step
    size, mask = lax.axis_size("ctx"), (1 << width) - 1

    def needed(source, m):
        mine = (source >> shift) & mask
        return not last or mine < mine ^ m

    return [
        lax.ppermute(send, "ctx", [(i, i ^ (m << shift)) for i in range(size) if needed(i, m)])
        for m in range(1, mask + 1)
    ]


def weights_of(step, others):
    mine = digit_of(step)
    at = [mine ^ (m + 1) for m in range(len(others))]
    zero = jnp.zeros_like(others[0])
    before = []
    for a in at:
        between = zero
        for b, other in zip(at, others):
            between = between + jnp.where((a < b) & (b < mine), other, 0.0)
        before.append(jnp.where(a < mine, jnp.exp(between), 0.0))
    return mine, at, before


def join(z, step, part, total, got, sums, carried=None):
    h0, count = part
    dh, parts = z.dh, len(got)

    def kernel(*refs):
        total_ref, sums_ref = refs[:2]
        got_refs = refs[2 : 2 + parts]
        carried_ref = refs[2 + parts] if carried is not None else None
        new_total, new_carried, send, new_sums = refs[-4:]
        if carried is None:
            own = jnp.broadcast_to(sums_ref[:, z.seg - 1 : z.seg], (PAD, LANES))
            ahead = jnp.zeros((PAD, LANES), F32)
        else:
            own, ahead = sums_ref[:PAD, :], sums_ref[PAD:, :]
        others = [get_sums(ref, count * dh) for ref in got_refs]
        mine, at, before = weights_of(step, others)
        whole, passed = own, jnp.zeros((PAD, LANES), F32)
        keep = jnp.zeros((PAD, LANES), F32)
        takes = []
        for a, other in zip(at, others):
            whole = whole + other
            passed = passed + jnp.where(a < mine, other, 0.0)
            keep = keep + jnp.where(a > mine, other, 0.0)
            behind = jnp.where(mine > a, own, 0.0)
            for b, third in zip(at, others):
                behind = behind + jnp.where(b > a, third, 0.0)
            takes.append(jnp.exp(behind))
        keep, lead = jnp.exp(keep), jnp.exp(ahead)
        for h in range(count):
            rows = slice(h * dh, (h + 1) * dh)
            row = slice(h0 + h, h0 + h + 1)
            value = total_ref[rows, :] * keep[row, :]
            moved = jnp.zeros((dh, dh), F32)
            for ref, take, weight in zip(got_refs, takes, before):
                theirs = ref[rows, :].astype(F32)
                value = value + theirs * take[row, :]
                moved = moved + theirs * (weight * lead)[row, :]
            new_total[rows, :] = value
            send[rows, :] = value.astype(BF16)
            new_carried[rows, :] = moved if carried is None else carried_ref[rows, :] + moved
        put_sums(send, count * dh, whole)
        new_sums[:PAD, :] = whole
        new_sums[PAD:, :] = ahead + passed

    shapes = [((count * dh, dh), F32)] * 2 + [((count * dh + 2 * PAD, dh), BF16), ((2 * PAD, LANES), F32)]
    args = [total, sums, *got] + ([] if carried is None else [carried])
    return call(kernel, shapes, args)


def attend(z, part, kv, qs_in, col, row, carried, got, sums):
    h0, count = part
    n, rows, dh, seg = z.n, z.rows, z.dh, z.seg

    def kernel(*refs):
        kv_refs, q_refs = refs[:n], refs[n : 2 * n]
        col_ref, row_ref, carried_ref, sums_ref = refs[2 * n : 2 * n + 4]
        got_refs = refs[2 * n + 4 : 2 * n + 4 + len(got)]
        outs = refs[-n - 4 : -4]
        ks, vs, qs, mixed = refs[-4:]
        scatter_heads(z, kv_refs, ks, h0, count)
        scatter_heads(z, kv_refs, vs, z.local + h0, count)
        scatter_heads(z, q_refs, qs, h0, count)
        before = weights_of(z.steps[-1], [get_sums(ref, count * dh) for ref in got_refs])[2]
        lead = jnp.exp(sums_ref[PAD:, :])
        before = [weight * lead for weight in before]
        t = lax.broadcasted_iota(jnp.int32, (seg, seg), 0)
        s = lax.broadcasted_iota(jnp.int32, (seg, seg), 1)
        causal = s <= t
        for h in range(count):
            at = slice(h * dh, (h + 1) * dh)
            former = carried_ref[at, :]
            for ref, weight in zip(got_refs, before):
                former = former + ref[at, :].astype(F32) * weight[h0 + h : h0 + h + 1, :]
            q = qs[h]
            d_col = col_ref[:, h0 + h : h0 + h + 1]
            scores = dot(q, ks[h], (1, 1))
            gap = jnp.where(causal, d_col - row_ref[h0 + h : h0 + h + 1, :], 0.0)
            weights = jnp.where(causal, scores * jnp.exp(gap), 0.0).astype(BF16)
            out = dot(weights, vs[h], (1, 0)) + jnp.exp(d_col) * dot(q, former.astype(BF16), (1, 0))
            mixed[:, at] = out.astype(BF16)
        me = lax.axis_index("inner")
        for k in range(n):
            chunk = lax.rem(me + k, n)
            outs[k][...] = mixed[pl.ds(pl.multiple_of(chunk * rows, rows), rows), :]

    scratch = [pltpu.VMEM((count, seg, dh), BF16)] * 3 + [pltpu.VMEM((seg, count * dh), BF16)]
    args = [*kv, *qs_in, col, row, carried, sums, *got]
    return call(kernel, [((rows, count * dh), BF16)] * n, args, scratch=scratch)


def normalize(z, lengths, gain, blocks):
    n, rows, dh = z.n, z.rows, z.dh

    def kernel(len_ref, gain_ref, *refs):
        out = refs[-1]
        me = lax.axis_index("inner")
        live = live_mask(len_ref, rows)
        total = jnp.zeros((rows, 1), F32)
        for ref in refs[:-1]:
            flat = ref[...].astype(F32)
            total = total + jnp.sum(flat * flat, axis=1, keepdims=True)
        inv = lax.rsqrt(total / z.width + 1e-06)
        for p, (h0, count) in enumerate(z.parts):
            for k in range(n):
                group = lax.rem(me + (n - k), n)
                cols = pl.ds(pl.multiple_of((group * z.local + h0) * dh, LANES), count * dh)
                scaled = refs[p * n + k][...].astype(F32) * inv * gain_ref[:, cols]
                out[:, cols] = jnp.where(live, scaled, 0.0).astype(BF16)

    flat_blocks = [block for part in blocks for block in part]
    args = [lengths, gain, *flat_blocks]
    specs = [SMEM] + [pl.BlockSpec(memory_space=pltpu.VMEM)] * (len(args) - 1)
    return call(kernel, [((rows, z.width), BF16)], args, specs)[0]


def shift_blocks(z, blocks):
    n = z.n
    return [blocks[0]] + [
        lax.ppermute(blocks[k], "inner", [(i, (i + k) % n) for i in range(n)]) for k in range(1, n)
    ]


def shards(low_rank, q_base, k_base, v_base, edit_up, log_decay, lengths, norm_gain):
    z = Sizes(q_base, log_decay)
    every = (0, z.local)
    low_rank, log_decay = low_rank.T, log_decay.T
    kv = project(z, "kv", every, lengths, low_rank, (k_base, v_base), edit_up, (1, 2), log_decay, True)
    kv = shift_blocks(z, kv)
    qs = project(z, "q", every, lengths, low_rank, (q_base,), edit_up, (0,), log_decay, False)
    qs = shift_blocks(z, [qs[0], *gate(qs[1:], (kv[1],))])
    col, row, *states = segment_states(z, kv)
    outs = []
    for p, part in enumerate(z.parts):
        total, send = states[2 * p : 2 * p + 2]
        carried, sums = None, row
        for step in z.steps[:-1]:
            got = exchange(step, False, send)
            total, carried, send, sums = join(z, step, part, total, got, sums, carried)
        got = exchange(z.steps[-1], True, send)
        outs.append(shift_blocks(z, attend(z, part, kv, qs, col, row, carried, got, sums)))
    return normalize(z, lengths, norm_gain[None, :], outs)


def solution(mesh):
    rows = P(("ctx", "inner"), None)
    return jax.shard_map(
        shards,
        mesh=mesh,
        in_specs=(rows, rows, rows, rows, P(), rows, P("ctx"), P()),
        out_specs=rows,
        check_vma=False,
    )
```

```python
import jax
import jax.numpy as jnp
from jax import lax
from jax.experimental import pallas as pl
from jax.experimental.pallas import tpu as pltpu
from jax.sharding import PartitionSpec as P

F32, BF16 = jnp.float32, jnp.bfloat16
LANES = 128
PAD = 16
PARTS = 2
PARAMS = pltpu.CompilerParams(vmem_limit_bytes=48 * 1024 * 1024)
COST = pl.CostEstimate(flops=1000000000, bytes_accessed=1, transcendentals=0)
SMEM = pl.BlockSpec(memory_space=pltpu.SMEM)


def dot(a, b, dims):
    return lax.dot_general(a, b, ((dims[:1], dims[1:]), ((), ())), preferred_element_type=F32)


def call(kernel, shapes, args, specs=None, scratch=(), after=()):
    whole = [pl.BlockSpec(memory_space=pltpu.VMEM)] * len(args) if specs is None else specs
    if after:
        inner, used = kernel, len(args)

        def kernel(*refs):
            inner(*refs[:used], *refs[used + len(after) :])

        args = [*args, *after]
        whole = [*whole, *([pl.BlockSpec(memory_space=pl.ANY)] * len(after))]
    return pl.pallas_call(
        kernel,
        out_shape=[jax.ShapeDtypeStruct(*shape) for shape in shapes],
        in_specs=whole,
        out_specs=[pl.BlockSpec(memory_space=pltpu.VMEM)] * len(shapes),
        scratch_shapes=list(scratch),
        compiler_params=PARAMS,
        cost_estimate=COST,
    )(*args)


def gate(arrays, after):
    every = pl.BlockSpec(memory_space=pl.ANY)
    return pl.pallas_call(
        lambda *refs: None,
        out_shape=[jax.ShapeDtypeStruct(a.shape, a.dtype) for a in arrays],
        in_specs=[every] * (len(arrays) + len(after)),
        out_specs=[every] * len(arrays),
        input_output_aliases={i: i for i in range(len(arrays))},
        compiler_params=PARAMS,
    )(*arrays, *after)


def live_mask(len_ref, rows):
    at = lax.axis_index("inner") * rows + lax.broadcasted_iota(jnp.int32, (rows, 1), 0)
    return at < len_ref[0]


class Sizes:
    def __init__(self, q_base, log_decay):
        self.n = lax.axis_size("inner")
        self.rows, self.width = q_base.shape
        self.heads = log_decay.shape[1]
        self.local = self.heads // self.n
        self.dh = self.width // self.heads
        self.seg = self.rows * self.n
        bits = (lax.axis_size("ctx") - 1).bit_length()
        self.steps = [(at, 1) for at in range(bits)]
        first = -(-self.local // PARTS)
        self.parts = []
        at = 0
        while at < self.local:
            self.parts.append((at, min(first, self.local - at)))
            at += first


def project(z, names, part, lengths, low_rank, bases, edit_up, columns, log_decay, decays, after=(), whole=False, places=None):
    h0, count = part
    n, rows, dh = z.n, z.rows, z.dh
    kinds = len(bases)
    rank = edit_up.shape[0]
    places = places or (*range(1, n), 0)
    height = kinds * count * rows + (PAD if decays else 0)

    def kernel(len_ref, lr_ref, *refs):
        base_refs, up_ref, ld_from = refs[:kinds], refs[kinds], refs[kinds + 1]
        me = lax.axis_index("inner")
        if whole:
            outs = [refs[-6].at[lax.rem(me + k, n)] for k in places]
        else:
            outs = refs[-len(places) - 5 : -5]
        base_buf, up_buf, low_buf, ld_ref, sems = refs[-5:]

        def copies(i):
            at = (lax.rem(me + places[i], n) * z.local + h0) * dh
            for kind in range(kinds):
                cols = pl.ds(pl.multiple_of(at, LANES), count * dh)
                up_cols = pl.ds(pl.multiple_of(at + columns[kind] * z.width, LANES), count * dh)
                slot = i * kinds + kind
                yield pltpu.make_async_copy(base_refs[kind].at[:, cols], base_buf.at[slot], sems.at[0, slot])
                yield pltpu.make_async_copy(up_ref.at[:, up_cols], up_buf.at[slot], sems.at[1, slot])

        small = [
            pltpu.make_async_copy(lr_ref, low_buf, sems.at[0, n * kinds]),
            pltpu.make_async_copy(ld_from, ld_ref, sems.at[1, n * kinds]),
        ]
        for copy in small:
            copy.start()
        for i in range(len(places)):
            for copy in copies(i):
                copy.start()
        live = live_mask(len_ref, rows)
        for copy in small:
            copy.wait()
        low = low_buf[...].T
        for i, k in enumerate(places):
            for copy in copies(i):
                copy.wait()
            for kind in range(kinds):
                slot = i * kinds + kind
                edited = base_buf[slot].astype(F32) + dot(low, up_buf[slot], (1, 0))
                if names[kind] != "q":
                    edited = jnp.where(live, edited, 0.0)
                edited = edited.astype(BF16)
                for h in range(count):
                    top = (kind * count + h) * rows
                    outs[i][top : top + rows, :] = edited[:, h * dh : (h + 1) * dh]
            if decays:
                row = lax.broadcasted_iota(jnp.int32, (PAD, z.heads), 0)
                col = lax.broadcasted_iota(jnp.int32, (PAD, z.heads), 1)
                group = lax.rem(me + k, n)
                pick = jnp.where((row < z.local) & (col == row + group * z.local), 1.0, 0.0).astype(BF16)
                wide = jnp.concatenate(
                    [dot(pick, ld_ref[...], (1, 0)), jnp.zeros((PAD, LANES - rows), F32)], axis=1
                )
                outs[i][height - PAD : height, :] = wide.astype(BF16)

    args = [lengths, *(pltpu.with_memory_space_constraint(a, pltpu.HBM) for a in (low_rank, *bases, edit_up, log_decay))]
    specs = [SMEM, *([pl.BlockSpec(memory_space=pltpu.HBM)] * (kinds + 3))]
    scratch = [
        pltpu.VMEM((n * kinds, rows, count * dh), BF16),
        pltpu.VMEM((n * kinds, rank, count * dh), BF16),
        pltpu.VMEM(low_rank.shape, BF16),
        pltpu.VMEM(log_decay.shape, BF16),
        pltpu.SemaphoreType.DMA((2, n * kinds + 1)),
    ]
    shapes = [((n, height, dh), BF16)] if whole else [((height, dh), BF16)] * len(places)
    return call(kernel, shapes, args, specs, scratch, after)


def scatter_heads(z, refs, held, first, count):
    me = lax.axis_index("inner")
    for k in range(z.n):
        chunk = lax.rem(me + (z.n - k), z.n)
        at = pl.ds(pl.multiple_of(chunk * z.rows, z.rows), z.rows)
        for h in range(count):
            top = (first + h) * z.rows
            held[h, at, :] = refs[k][top : top + z.rows, :]


def segment_states(z, part, kv, decays=None, after=()):
    h0, count = part
    n, rows, dh, seg = z.n, z.rows, z.dh, z.seg
    first = decays is None

    def kernel(*refs):
        kv_refs, refs = refs[:n], refs[n:]
        if first:
            state, send, col_ref, row_ref, ks, vs, lds = refs
        else:
            col_ref, row_ref, state, send, ks, vs = refs
        if first:
            me = lax.axis_index("inner")
            for k in range(n):
                lds[lax.rem(me + (n - k), n)] = kv_refs[k][2 * z.local * rows :, :]
            t = lax.broadcasted_iota(jnp.int32, (rows, LANES), 0)
            s = lax.broadcasted_iota(jnp.int32, (rows, LANES), 1)
            tri = jnp.where(s <= t, 1.0, 0.0).astype(BF16)
            so_far = jnp.zeros((1, PAD), F32)
            for j in range(n):
                cum = dot(tri, lds[j], (1, 1)) + so_far
                so_far = cum[rows - 1 : rows, :]
                wide = jnp.concatenate([cum, jnp.zeros((rows, LANES - PAD), F32)], axis=1)
                col_ref[j * rows : (j + 1) * rows, :] = wide
            row_ref[...] = col_ref[...].T[:PAD, :]
        scatter_heads(z, kv_refs, ks, h0, count)
        scatter_heads(z, kv_refs, vs, z.local + h0, count)
        col = col_ref[...]
        scale = jnp.exp(col[seg - 1 : seg, :] - col)
        for h in range(count):
            scaled = (ks[h].astype(F32) * scale[:, h0 + h : h0 + h + 1]).astype(BF16)
            value = dot(scaled, vs[h], (0, 0))
            state[h * dh : (h + 1) * dh, :] = value
            send[h * dh : (h + 1) * dh, :] = value.astype(BF16)
        put_sums(send, count * dh, jnp.broadcast_to(row_ref[:, seg - 1 : seg], (PAD, LANES)))

    shapes = [((count * dh, dh), F32), ((count * dh + 2 * PAD, dh), BF16)]
    scratch = [pltpu.VMEM((count, seg, dh), BF16)] * 2
    if first:
        shapes += [((seg, LANES), F32), ((PAD, seg), F32)]
        scratch.append(pltpu.VMEM((n, PAD, LANES), BF16))
    return call(kernel, shapes, [*kv, *(decays or ())], scratch=scratch, after=after)


def put_sums(send, at, sums):
    high = sums.astype(BF16)
    send[at : at + PAD, :] = high
    send[at + PAD : at + 2 * PAD, :] = (sums - high.astype(F32)).astype(BF16)


def get_sums(got, at):
    return got[at : at + PAD, :].astype(F32) + got[at + PAD : at + 2 * PAD, :].astype(F32)


def digit_of(step):
    shift, width = step
    return lax.rem(lax.axis_index("ctx") // (1 << shift), 1 << width)


def exchange(step, last, send):
    shift, width = step
    size, mask = lax.axis_size("ctx"), (1 << width) - 1

    def needed(source, m):
        mine = (source >> shift) & mask
        return not last or mine < mine ^ m

    return [
        lax.ppermute(send, "ctx", [(i, i ^ (m << shift)) for i in range(size) if needed(i, m)])
        for m in range(1, mask + 1)
    ]


def weights_of(step, others):
    mine = digit_of(step)
    at = [mine ^ (m + 1) for m in range(len(others))]
    zero = jnp.zeros_like(others[0])
    before = []
    for a in at:
        between = zero
        for b, other in zip(at, others):
            between = between + jnp.where((a < b) & (b < mine), other, 0.0)
        before.append(jnp.where(a < mine, jnp.exp(between), 0.0))
    return mine, at, before


def join(z, step, part, total, got, sums, carried=None, final=False):
    h0, count = part
    dh, parts = z.dh, len(got)

    def kernel(*refs):
        total_ref, sums_ref = refs[:2]
        got_refs = refs[2 : 2 + parts]
        carried_ref = refs[2 + parts] if carried is not None else None
        new_carried, send, new_sums = refs[-3:]
        new_total = None if final else refs[-4]
        if carried is None:
            own = jnp.broadcast_to(sums_ref[:, z.seg - 1 : z.seg], (PAD, LANES))
            ahead = jnp.zeros((PAD, LANES), F32)
        else:
            own, ahead = sums_ref[:PAD, :], sums_ref[PAD:, :]
        others = [get_sums(ref, count * dh) for ref in got_refs]
        mine, at, before = weights_of(step, others)
        whole, passed = own, jnp.zeros((PAD, LANES), F32)
        keep = jnp.zeros((PAD, LANES), F32)
        takes = []
        for a, other in zip(at, others):
            whole = whole + other
            passed = passed + jnp.where(a < mine, other, 0.0)
            keep = keep + jnp.where(a > mine, other, 0.0)
            behind = jnp.where(mine > a, own, 0.0)
            for b, third in zip(at, others):
                behind = behind + jnp.where(b > a, third, 0.0)
            takes.append(jnp.exp(behind))
        keep, lead = jnp.exp(keep), jnp.exp(ahead)
        for h in range(count):
            rows = slice(h * dh, (h + 1) * dh)
            row = slice(h0 + h, h0 + h + 1)
            value = total_ref[rows, :] * keep[row, :]
            moved = jnp.zeros((dh, dh), F32)
            for ref, take, weight in zip(got_refs, takes, before):
                theirs = ref[rows, :].astype(F32)
                value = value + theirs * take[row, :]
                moved = moved + theirs * (weight * lead)[row, :]
            if not final:
                new_total[rows, :] = value
            send[rows, :] = value.astype(BF16)
            new_carried[rows, :] = moved if carried is None else carried_ref[rows, :] + moved
        put_sums(send, count * dh, whole)
        new_sums[:PAD, :] = whole
        new_sums[PAD:, :] = ahead + passed

    shapes = [((count * dh, dh), F32)] * (1 if final else 2)
    shapes += [((count * dh + 2 * PAD, dh), BF16), ((2 * PAD, LANES), F32)]
    args = [total, sums, *got] + ([] if carried is None else [carried])
    return call(kernel, shapes, args)


def attend(z, part, kv, qs_in, col, row, carried, got, sums):
    h0, count = part
    n, rows, dh, seg = z.n, z.rows, z.dh, z.seg

    def kernel(*refs):
        kv_refs, q_refs = refs[:n], refs[n : n + 1]
        col_ref, row_ref, carried_ref, sums_ref = refs[n + 1 : n + 5]
        got_refs = refs[n + 5 : n + 5 + len(got)]
        outs = refs[-n - 4 : -4]
        ks, vs, qs, mixed = refs[-4:]
        scatter_heads(z, kv_refs, ks, h0, count)
        scatter_heads(z, kv_refs, vs, z.local + h0, count)
        for chunk in range(n):
            for h in range(count):
                rows_of = slice((h0 + h) * rows, (h0 + h + 1) * rows)
                qs[h, chunk * rows : (chunk + 1) * rows, :] = q_refs[0][chunk, rows_of, :]
        before = weights_of(z.steps[-1], [get_sums(ref, count * dh) for ref in got_refs])[2]
        lead = jnp.exp(sums_ref[PAD:, :])
        before = [weight * lead for weight in before]
        t = lax.broadcasted_iota(jnp.int32, (seg, seg), 0)
        s = lax.broadcasted_iota(jnp.int32, (seg, seg), 1)
        causal = s <= t
        for h in range(count):
            at = slice(h * dh, (h + 1) * dh)
            former = carried_ref[at, :]
            for ref, weight in zip(got_refs, before):
                former = former + ref[at, :].astype(F32) * weight[h0 + h : h0 + h + 1, :]
            q = qs[h]
            d_col = col_ref[:, h0 + h : h0 + h + 1]
            scores = dot(q, ks[h], (1, 1))
            gap = jnp.where(causal, d_col - row_ref[h0 + h : h0 + h + 1, :], 0.0)
            weights = jnp.where(causal, scores * jnp.exp(gap), 0.0).astype(BF16)
            out = dot(weights, vs[h], (1, 0)) + jnp.exp(d_col) * dot(q, former.astype(BF16), (1, 0))
            mixed[:, at] = out.astype(BF16)
        me = lax.axis_index("inner")
        for k in range(n):
            chunk = lax.rem(me + k, n)
            outs[k][...] = mixed[pl.ds(pl.multiple_of(chunk * rows, rows), rows), :]

    scratch = [pltpu.VMEM((count, seg, dh), BF16)] * 3 + [pltpu.VMEM((seg, count * dh), BF16)]
    args = [*kv, *qs_in, col, row, carried, sums, *got]
    return call(kernel, [((rows, count * dh), BF16)] * n, args, scratch=scratch)


def normalize(z, lengths, gain, blocks):
    n, rows, dh = z.n, z.rows, z.dh

    def kernel(len_ref, gain_ref, *refs):
        out = refs[-1]
        me = lax.axis_index("inner")
        live = live_mask(len_ref, rows)
        total = jnp.zeros((rows, 1), F32)
        for ref in refs[:-1]:
            flat = ref[...].astype(F32)
            total = total + jnp.sum(flat * flat, axis=1, keepdims=True)
        inv = lax.rsqrt(total / z.width + 1e-06)
        for p, (h0, count) in enumerate(z.parts):
            for k in range(n):
                group = lax.rem(me + (n - k), n)
                cols = pl.ds(pl.multiple_of((group * z.local + h0) * dh, LANES), count * dh)
                scaled = refs[p * n + k][...].astype(F32) * inv * gain_ref[:, cols]
                out[:, cols] = jnp.where(live, scaled, 0.0).astype(BF16)

    flat_blocks = [block for part in blocks for block in part]
    args = [lengths, gain, *flat_blocks]
    specs = [SMEM] + [pl.BlockSpec(memory_space=pltpu.VMEM)] * (len(args) - 1)
    return call(kernel, [((rows, z.width), BF16)], args, specs)[0]


def shift_blocks(z, blocks):
    n = z.n
    return [blocks[0]] + [
        lax.ppermute(blocks[k], "inner", [(i, (i + k) % n) for i in range(n)]) for k in range(1, n)
    ]


def shards(low_rank, q_base, k_base, v_base, edit_up, log_decay, lengths, norm_gain):
    z = Sizes(q_base, log_decay)
    every = (0, z.local)
    low_rank, log_decay = low_rank.T, log_decay.T
    kv = [None] * z.n
    first = z.n // 2
    for ks in ((first,), tuple(k for k in range(1, z.n) if k != first) + (0,)):
        made = project(
            z, "kv", every, lengths, low_rank, (k_base, v_base), edit_up, (1, 2), log_decay, True, places=ks
        )
        for k, block in zip(ks, made):
            kv[k] = block
    kv = shift_blocks(z, kv)
    qs = project(z, "q", every, lengths, low_rank, (q_base,), edit_up, (0,), log_decay, False, whole=True)
    qs = gate(qs, (kv[2],))
    qs = [lax.all_to_all(qs[0], "inner", split_axis=0, concat_axis=0, tiled=True)]
    outs = []
    decays = None
    for p, part in enumerate(z.parts):
        total, send, *made = segment_states(z, part, kv, decays)
        decays = decays or made
        carried, sums = None, decays[1]
        for step in z.steps[:-1]:
            final = step is z.steps[-2]
            got = exchange(step, False, send)
            *total, carried, send, sums = join(z, step, part, total, got, sums, carried, final)
            total = total[0] if total else None
        got = exchange(z.steps[-1], True, send)
        outs.append(shift_blocks(z, attend(z, part, kv, qs, *decays, carried, got, sums)))
    return normalize(z, lengths, norm_gain[None, :], outs)


def solution(mesh):
    rows = P(("ctx", "inner"), None)
    return jax.shard_map(
        shards,
        mesh=mesh,
        in_specs=(rows, rows, rows, rows, P(), rows, P("ctx"), P()),
        out_specs=rows,
        check_vma=False,
    )
```

```python
import jax
import jax.numpy as jnp
from jax import lax
from jax.experimental import pallas as pl
from jax.experimental.pallas import tpu as pltpu
from jax.sharding import PartitionSpec as P

F32, BF16 = jnp.float32, jnp.bfloat16
LANES = 128
PAD = 16
PARTS = 2
PARAMS = pltpu.CompilerParams(vmem_limit_bytes=48 * 1024 * 1024)
COST = pl.CostEstimate(flops=1000000000, bytes_accessed=1, transcendentals=0)
SMEM = pl.BlockSpec(memory_space=pltpu.SMEM)


def dot(a, b, dims):
    return lax.dot_general(a, b, ((dims[:1], dims[1:]), ((), ())), preferred_element_type=F32)


def call(kernel, shapes, args, specs=None, scratch=(), after=()):
    whole = [pl.BlockSpec(memory_space=pltpu.VMEM)] * len(args) if specs is None else specs
    if after:
        inner, used = kernel, len(args)

        def kernel(*refs):
            inner(*refs[:used], *refs[used + len(after) :])

        args = [*args, *after]
        whole = [*whole, *([pl.BlockSpec(memory_space=pl.ANY)] * len(after))]
    return pl.pallas_call(
        kernel,
        out_shape=[jax.ShapeDtypeStruct(*shape) for shape in shapes],
        in_specs=whole,
        out_specs=[pl.BlockSpec(memory_space=pltpu.VMEM)] * len(shapes),
        scratch_shapes=list(scratch),
        compiler_params=PARAMS,
        cost_estimate=COST,
    )(*args)


def gate(arrays, after):
    every = pl.BlockSpec(memory_space=pl.ANY)
    return pl.pallas_call(
        lambda *refs: None,
        out_shape=[jax.ShapeDtypeStruct(a.shape, a.dtype) for a in arrays],
        in_specs=[every] * (len(arrays) + len(after)),
        out_specs=[every] * len(arrays),
        input_output_aliases={i: i for i in range(len(arrays))},
        compiler_params=PARAMS,
    )(*arrays, *after)


def live_mask(len_ref, rows):
    at = lax.axis_index("inner") * rows + lax.broadcasted_iota(jnp.int32, (rows, 1), 0)
    return at < len_ref[0]


class Sizes:
    def __init__(self, q_base, log_decay):
        self.n = lax.axis_size("inner")
        self.rows, self.width = q_base.shape
        self.heads = log_decay.shape[1]
        self.local = self.heads // self.n
        self.dh = self.width // self.heads
        self.seg = self.rows * self.n
        bits = (lax.axis_size("ctx") - 1).bit_length()
        self.steps = [(at, 1) for at in range(bits)]
        first = max(1, self.local // PARTS)
        self.parts = [(at, min(first, self.local - at)) for at in range(0, first * PARTS, first) if at < self.local]
        self.parts[-1] = (self.parts[-1][0], self.local - self.parts[-1][0])


def project(z, names, part, lengths, low_rank, bases, edit_up, columns, log_decay, decays, after=(), whole=False, places=None):
    h0, count = part
    n, rows, dh = z.n, z.rows, z.dh
    kinds = len(bases)
    rank = edit_up.shape[0]
    places = places or (*range(1, n), 0)
    height = kinds * count * rows + (PAD if decays else 0)

    def kernel(len_ref, lr_ref, *refs):
        base_refs, up_ref, ld_from = refs[:kinds], refs[kinds], refs[kinds + 1]
        me = lax.axis_index("inner")
        if whole:
            outs = [refs[-6].at[lax.rem(me + k, n)] for k in places]
        else:
            outs = refs[-len(places) - 5 : -5]
        base_buf, up_buf, low_buf, ld_ref, sems = refs[-5:]

        def copies(i):
            at = (lax.rem(me + places[i], n) * z.local + h0) * dh
            for kind in range(kinds):
                cols = pl.ds(pl.multiple_of(at, LANES), count * dh)
                up_cols = pl.ds(pl.multiple_of(at + columns[kind] * z.width, LANES), count * dh)
                slot = i * kinds + kind
                yield pltpu.make_async_copy(base_refs[kind].at[:, cols], base_buf.at[slot], sems.at[0, slot])
                yield pltpu.make_async_copy(up_ref.at[:, up_cols], up_buf.at[slot], sems.at[1, slot])

        small = [
            pltpu.make_async_copy(lr_ref, low_buf, sems.at[0, n * kinds]),
            pltpu.make_async_copy(ld_from, ld_ref, sems.at[1, n * kinds]),
        ]
        for copy in small:
            copy.start()
        for i in range(len(places)):
            for copy in copies(i):
                copy.start()
        live = live_mask(len_ref, rows)
        for copy in small:
            copy.wait()
        low = low_buf[...].T
        for i, k in enumerate(places):
            for copy in copies(i):
                copy.wait()
            for kind in range(kinds):
                slot = i * kinds + kind
                edited = base_buf[slot].astype(F32) + dot(low, up_buf[slot], (1, 0))
                if names[kind] != "q":
                    edited = jnp.where(live, edited, 0.0)
                edited = edited.astype(BF16)
                for h in range(count):
                    top = (kind * count + h) * rows
                    outs[i][top : top + rows, :] = edited[:, h * dh : (h + 1) * dh]
            if decays:
                row = lax.broadcasted_iota(jnp.int32, (PAD, z.heads), 0)
                col = lax.broadcasted_iota(jnp.int32, (PAD, z.heads), 1)
                group = lax.rem(me + k, n)
                pick = jnp.where((row < z.local) & (col == row + group * z.local), 1.0, 0.0).astype(BF16)
                wide = jnp.concatenate(
                    [dot(pick, ld_ref[...], (1, 0)), jnp.zeros((PAD, LANES - rows), F32)], axis=1
                )
                outs[i][height - PAD : height, :] = wide.astype(BF16)

    args = [lengths, *(pltpu.with_memory_space_constraint(a, pltpu.HBM) for a in (low_rank, *bases, edit_up, log_decay))]
    specs = [SMEM, *([pl.BlockSpec(memory_space=pltpu.HBM)] * (kinds + 3))]
    scratch = [
        pltpu.VMEM((n * kinds, rows, count * dh), BF16),
        pltpu.VMEM((n * kinds, rank, count * dh), BF16),
        pltpu.VMEM(low_rank.shape, BF16),
        pltpu.VMEM(log_decay.shape, BF16),
        pltpu.SemaphoreType.DMA((2, n * kinds + 1)),
    ]
    shapes = [((n, height, dh), BF16)] if whole else [((height, dh), BF16)] * len(places)
    return call(kernel, shapes, args, specs, scratch, after)


def scatter_heads(z, refs, held, first, count):
    me = lax.axis_index("inner")
    for k in range(z.n):
        chunk = lax.rem(me + (z.n - k), z.n)
        at = pl.ds(pl.multiple_of(chunk * z.rows, z.rows), z.rows)
        for h in range(count):
            top = (first + h) * z.rows
            held[h, at, :] = refs[k][top : top + z.rows, :]


def segment_states(z, part, kv, decays=None, after=()):
    h0, count = part
    n, rows, dh, seg = z.n, z.rows, z.dh, z.seg
    first = decays is None

    def kernel(*refs):
        kv_refs, refs = refs[:n], refs[n:]
        if first:
            state, send, col_ref, row_ref, ks, vs, lds = refs
        else:
            col_ref, row_ref, state, send, ks, vs = refs
        if first:
            me = lax.axis_index("inner")
            for k in range(n):
                lds[lax.rem(me + (n - k), n)] = kv_refs[k][2 * z.local * rows :, :]
            t = lax.broadcasted_iota(jnp.int32, (rows, LANES), 0)
            s = lax.broadcasted_iota(jnp.int32, (rows, LANES), 1)
            tri = jnp.where(s <= t, 1.0, 0.0).astype(BF16)
            so_far = jnp.zeros((1, PAD), F32)
            for j in range(n):
                cum = dot(tri, lds[j], (1, 1)) + so_far
                so_far = cum[rows - 1 : rows, :]
                wide = jnp.concatenate([cum, jnp.zeros((rows, LANES - PAD), F32)], axis=1)
                col_ref[j * rows : (j + 1) * rows, :] = wide
            row_ref[...] = col_ref[...].T[:PAD, :]
        scatter_heads(z, kv_refs, ks, h0, count)
        scatter_heads(z, kv_refs, vs, z.local + h0, count)
        col = col_ref[...]
        scale = jnp.exp(col[seg - 1 : seg, :] - col)
        for h in range(count):
            scaled = (ks[h].astype(F32) * scale[:, h0 + h : h0 + h + 1]).astype(BF16)
            value = dot(scaled, vs[h], (0, 0))
            state[h * dh : (h + 1) * dh, :] = value
            send[h * dh : (h + 1) * dh, :] = value.astype(BF16)
        put_sums(send, count * dh, jnp.broadcast_to(row_ref[:, seg - 1 : seg], (PAD, LANES)))

    shapes = [((count * dh, dh), F32), ((count * dh + 2 * PAD, dh), BF16)]
    scratch = [pltpu.VMEM((count, seg, dh), BF16)] * 2
    if first:
        shapes += [((seg, LANES), F32), ((PAD, seg), F32)]
        scratch.append(pltpu.VMEM((n, PAD, LANES), BF16))
    return call(kernel, shapes, [*kv, *(decays or ())], scratch=scratch, after=after)


def put_sums(send, at, sums):
    high = sums.astype(BF16)
    send[at : at + PAD, :] = high
    send[at + PAD : at + 2 * PAD, :] = (sums - high.astype(F32)).astype(BF16)


def get_sums(got, at):
    return got[at : at + PAD, :].astype(F32) + got[at + PAD : at + 2 * PAD, :].astype(F32)


def digit_of(step):
    shift, width = step
    return lax.rem(lax.axis_index("ctx") // (1 << shift), 1 << width)


def exchange(step, send):
    shift, width = step
    size = lax.axis_size("ctx")
    return [
        lax.ppermute(send, "ctx", [(i, i ^ (m << shift)) for i in range(size)]) for m in range(1, 1 << width)
    ]


def weights_of(step, others):
    mine = digit_of(step)
    at = [mine ^ (m + 1) for m in range(len(others))]
    zero = jnp.zeros_like(others[0])
    before = []
    for a in at:
        between = zero
        for b, other in zip(at, others):
            between = between + jnp.where((a < b) & (b < mine), other, 0.0)
        before.append(jnp.where(a < mine, jnp.exp(between), 0.0))
    return mine, at, before


def join(z, step, part, total, got, sums, carried=None, final=False):
    h0, count = part
    dh, parts = z.dh, len(got)

    def kernel(*refs):
        total_ref, sums_ref = refs[:2]
        got_refs = refs[2 : 2 + parts]
        carried_ref = refs[2 + parts] if carried is not None else None
        new_carried, send, new_sums = refs[-3:]
        new_total = None if final else refs[-4]
        if carried is None:
            own = jnp.broadcast_to(sums_ref[:, z.seg - 1 : z.seg], (PAD, LANES))
            ahead = jnp.zeros((PAD, LANES), F32)
        else:
            own, ahead = sums_ref[:PAD, :], sums_ref[PAD:, :]
        others = [get_sums(ref, count * dh) for ref in got_refs]
        mine, at, before = weights_of(step, others)
        whole, passed = own, jnp.zeros((PAD, LANES), F32)
        keep = jnp.zeros((PAD, LANES), F32)
        takes = []
        for a, other in zip(at, others):
            whole = whole + other
            passed = passed + jnp.where(a < mine, other, 0.0)
            keep = keep + jnp.where(a > mine, other, 0.0)
            behind = jnp.where(mine > a, own, 0.0)
            for b, third in zip(at, others):
                behind = behind + jnp.where(b > a, third, 0.0)
            takes.append(jnp.exp(behind))
        keep, lead = jnp.exp(keep), jnp.exp(ahead)
        for h in range(count):
            rows = slice(h * dh, (h + 1) * dh)
            row = slice(h0 + h, h0 + h + 1)
            value = total_ref[rows, :] * keep[row, :]
            moved = jnp.zeros((dh, dh), F32)
            for ref, take, weight in zip(got_refs, takes, before):
                theirs = ref[rows, :].astype(F32)
                value = value + theirs * take[row, :]
                moved = moved + theirs * (weight * lead)[row, :]
            if not final:
                new_total[rows, :] = value
            send[rows, :] = value.astype(BF16)
            new_carried[rows, :] = moved if carried is None else carried_ref[rows, :] + moved
        put_sums(send, count * dh, whole)
        new_sums[:PAD, :] = whole
        new_sums[PAD:, :] = ahead + passed

    shapes = [((count * dh, dh), F32)] * (1 if final else 2)
    shapes += [((count * dh + 2 * PAD, dh), BF16), ((2 * PAD, LANES), F32)]
    args = [total, sums, *got] + ([] if carried is None else [carried])
    return call(kernel, shapes, args)


def attend(z, part, kv, qs_in, col, row, carried, got, sums):
    h0, count = part
    n, rows, dh, seg = z.n, z.rows, z.dh, z.seg

    def kernel(*refs):
        kv_refs, q_refs = refs[:n], refs[n : n + 1]
        col_ref, row_ref, carried_ref, sums_ref = refs[n + 1 : n + 5]
        got_refs = refs[n + 5 : n + 5 + len(got)]
        outs = refs[-n - 4 : -4]
        ks, vs, qs, mixed = refs[-4:]
        scatter_heads(z, kv_refs, ks, h0, count)
        scatter_heads(z, kv_refs, vs, z.local + h0, count)
        for chunk in range(n):
            for h in range(count):
                rows_of = slice((h0 + h) * rows, (h0 + h + 1) * rows)
                qs[h, chunk * rows : (chunk + 1) * rows, :] = q_refs[0][chunk, rows_of, :]
        before = weights_of(z.steps[-1], [get_sums(ref, count * dh) for ref in got_refs])[2]
        lead = jnp.exp(sums_ref[PAD:, :])
        before = [weight * lead for weight in before]
        t = lax.broadcasted_iota(jnp.int32, (seg, seg), 0)
        s = lax.broadcasted_iota(jnp.int32, (seg, seg), 1)
        causal = s <= t
        for h in range(count):
            at = slice(h * dh, (h + 1) * dh)
            former = carried_ref[at, :]
            for ref, weight in zip(got_refs, before):
                former = former + ref[at, :].astype(F32) * weight[h0 + h : h0 + h + 1, :]
            q = qs[h]
            d_col = col_ref[:, h0 + h : h0 + h + 1]
            scores = dot(q, ks[h], (1, 1))
            gap = jnp.where(causal, d_col - row_ref[h0 + h : h0 + h + 1, :], 0.0)
            weights = jnp.where(causal, scores * jnp.exp(gap), 0.0).astype(BF16)
            out = dot(weights, vs[h], (1, 0)) + jnp.exp(d_col) * dot(q, former.astype(BF16), (1, 0))
            mixed[:, at] = out.astype(BF16)
        me = lax.axis_index("inner")
        for k in range(n):
            chunk = lax.rem(me + k, n)
            outs[k][...] = mixed[pl.ds(pl.multiple_of(chunk * rows, rows), rows), :]

    scratch = [pltpu.VMEM((count, seg, dh), BF16)] * 3 + [pltpu.VMEM((seg, count * dh), BF16)]
    args = [*kv, *qs_in, col, row, carried, sums, *got]
    return call(kernel, [((rows, count * dh), BF16)] * n, args, scratch=scratch)


def squares(z, blocks):
    def kernel(*refs):
        total = jnp.zeros((z.rows, 1), F32)
        for ref in refs[:-1]:
            flat = ref[...].astype(F32)
            total = total + jnp.sum(flat * flat, axis=1, keepdims=True)
        refs[-1][...] = jnp.broadcast_to(total, (z.rows, LANES))

    return call(kernel, [((z.rows, LANES), F32)], blocks)[0]


def normalize(z, lengths, gain, blocks):
    n, rows, dh = z.n, z.rows, z.dh
    early = squares(z, [block for part in blocks[:-1] for block in part])

    def kernel(len_ref, gain_ref, early_ref, *refs):
        out = refs[-1]
        me = lax.axis_index("inner")
        live = live_mask(len_ref, rows)
        total = early_ref[:, :1]
        for ref in refs[-1 - n : -1]:
            flat = ref[...].astype(F32)
            total = total + jnp.sum(flat * flat, axis=1, keepdims=True)
        inv = lax.rsqrt(total / z.width + 1e-06)
        for p, (h0, count) in enumerate(z.parts):
            for k in range(n):
                group = lax.rem(me + (n - k), n)
                cols = pl.ds(pl.multiple_of((group * z.local + h0) * dh, LANES), count * dh)
                scaled = refs[p * n + k][...].astype(F32) * inv * gain_ref[:, cols]
                out[:, cols] = jnp.where(live, scaled, 0.0).astype(BF16)

    args = [lengths, gain, early, *(block for part in blocks for block in part)]
    specs = [SMEM] + [pl.BlockSpec(memory_space=pltpu.VMEM)] * (len(args) - 1)
    return call(kernel, [((rows, z.width), BF16)], args, specs)[0]


def shift_blocks(z, blocks):
    n = z.n
    return [blocks[0]] + [
        lax.ppermute(blocks[k], "inner", [(i, (i + k) % n) for i in range(n)]) for k in range(1, n)
    ]


def shards(low_rank, q_base, k_base, v_base, edit_up, log_decay, lengths, norm_gain):
    z = Sizes(q_base, log_decay)
    every = (0, z.local)
    low_rank, log_decay = low_rank.T, log_decay.T
    kv = [None] * z.n
    first = z.n // 2
    for ks in ((first,), tuple(k for k in range(1, z.n) if k != first) + (0,)):
        made = project(
            z, "kv", every, lengths, low_rank, (k_base, v_base), edit_up, (1, 2), log_decay, True, places=ks
        )
        for k, block in zip(ks, made):
            kv[k] = block
    kv = shift_blocks(z, kv)
    qs = project(z, "q", every, lengths, low_rank, (q_base,), edit_up, (0,), log_decay, False, whole=True)
    qs = gate(qs, (kv[first],))
    qs = [lax.all_to_all(qs[0], "inner", split_axis=0, concat_axis=0, tiled=True)]
    outs = []
    decays = None
    for p, part in enumerate(z.parts):
        total, send, *made = segment_states(z, part, kv, decays)
        decays = decays or made
        carried, sums = None, decays[1]
        for step in z.steps[:-1]:
            final = step is z.steps[-2]
            got = exchange(step, send)
            *total, carried, send, sums = join(z, step, part, total, got, sums, carried, final)
            total = total[0] if total else None
        got = exchange(z.steps[-1], send)
        outs.append(shift_blocks(z, attend(z, part, kv, qs, *decays, carried, got, sums)))
    return normalize(z, lengths, norm_gain[None, :], outs)


def solution(mesh):
    rows = P(("ctx", "inner"), None)
    return jax.shard_map(
        shards,
        mesh=mesh,
        in_specs=(rows, rows, rows, rows, P(), rows, P("ctx"), P()),
        out_specs=rows,
        check_vma=False,
    )
```

```python
import jax
import jax.numpy as jnp
from jax import lax
from jax.experimental import pallas as pl
from jax.experimental.pallas import tpu as pltpu
from jax.sharding import PartitionSpec as P

F32, BF16 = jnp.float32, jnp.bfloat16
LANES = 128
PAD = 16
PARTS = 2
PARAMS = pltpu.CompilerParams(vmem_limit_bytes=32 * 1024 * 1024)
COST = pl.CostEstimate(flops=1000000000, bytes_accessed=1, transcendentals=0)
SMEM = pl.BlockSpec(memory_space=pltpu.SMEM)


def dot(a, b, dims):
    return lax.dot_general(a, b, ((dims[:1], dims[1:]), ((), ())), preferred_element_type=F32)


def call(kernel, shapes, args, specs=None, scratch=(), after=(), out=pltpu.VMEM):
    whole = [pl.BlockSpec(memory_space=pltpu.VMEM)] * len(args) if specs is None else specs
    if after:
        inner, used = kernel, len(args)

        def kernel(*refs):
            inner(*refs[:used], *refs[used + len(after) :])

        args = [*args, *after]
        whole = [*whole, *([pl.BlockSpec(memory_space=pl.ANY)] * len(after))]
    return pl.pallas_call(
        kernel,
        out_shape=[jax.ShapeDtypeStruct(*shape) for shape in shapes],
        in_specs=whole,
        out_specs=[pl.BlockSpec(memory_space=out)] * len(shapes),
        scratch_shapes=list(scratch),
        compiler_params=PARAMS,
        cost_estimate=COST,
    )(*args)


def gate(arrays, after):
    every = pl.BlockSpec(memory_space=pl.ANY)
    return pl.pallas_call(
        lambda *refs: None,
        out_shape=[jax.ShapeDtypeStruct(a.shape, a.dtype) for a in arrays],
        in_specs=[every] * (len(arrays) + len(after)),
        out_specs=[every] * len(arrays),
        input_output_aliases={i: i for i in range(len(arrays))},
        compiler_params=PARAMS,
    )(*arrays, *after)


def live_mask(len_ref, rows):
    at = lax.axis_index("inner") * rows + lax.broadcasted_iota(jnp.int32, (rows, 1), 0)
    return at < len_ref[0]


class Sizes:
    def __init__(self, q_base, log_decay):
        self.n = lax.axis_size("inner")
        self.rows, self.width = q_base.shape
        self.heads = log_decay.shape[1]
        self.local = self.heads // self.n
        self.dh = self.width // self.heads
        self.seg = self.rows * self.n
        bits = (lax.axis_size("ctx") - 1).bit_length()
        self.steps = [(at, 1) for at in range(bits)]
        first = max(1, self.local // PARTS)
        self.parts = [(at, min(first, self.local - at)) for at in range(0, first * PARTS, first) if at < self.local]
        self.parts[-1] = (self.parts[-1][0], self.local - self.parts[-1][0])


def project(z, names, part, lengths, low_rank, bases, edit_up, columns, log_decay, decays, after=(), whole=False, places=None):
    h0, count = part
    n, rows, dh = z.n, z.rows, z.dh
    kinds = len(bases)
    rank = edit_up.shape[0]
    places = places or (*range(1, n), 0)
    height = kinds * count * rows + (PAD if decays else 0)

    def kernel(len_ref, lr_ref, *refs):
        base_refs, up_ref = refs[:kinds], refs[kinds]
        ld_ref = refs[kinds + 1] if decays else None
        me = lax.axis_index("inner")
        if whole:
            outs = [refs[-5].at[lax.rem(me + k, n)] for k in places]
        else:
            outs = refs[-len(places) - 4 : -4]
        base_buf, up_buf, low_buf, sems = refs[-4:]

        def copies(i):
            at = (lax.rem(me + places[i], n) * z.local + h0) * dh
            for kind in range(kinds):
                cols = pl.ds(pl.multiple_of(at, LANES), count * dh)
                up_cols = pl.ds(pl.multiple_of(at + columns[kind] * z.width, LANES), count * dh)
                slot = i * kinds + kind
                yield pltpu.make_async_copy(base_refs[kind].at[:, cols], base_buf.at[slot], sems.at[0, slot])
                yield pltpu.make_async_copy(up_ref.at[:, up_cols], up_buf.at[slot], sems.at[1, slot])

        small = pltpu.make_async_copy(lr_ref, low_buf, sems.at[0, n * kinds])
        small.start()
        for i in range(len(places)):
            for copy in copies(i):
                copy.start()
        live = live_mask(len_ref, rows)
        small.wait()
        low = low_buf[...].T
        for i, k in enumerate(places):
            for copy in copies(i):
                copy.wait()
            for kind in range(kinds):
                slot = i * kinds + kind
                edited = base_buf[slot].astype(F32) + dot(low, up_buf[slot], (1, 0))
                if names[kind] != "q":
                    edited = jnp.where(live, edited, 0.0)
                edited = edited.astype(BF16)
                for h in range(count):
                    top = (kind * count + h) * rows
                    outs[i][top : top + rows, :] = edited[:, h * dh : (h + 1) * dh]
            if decays:
                row = lax.broadcasted_iota(jnp.int32, (PAD, z.heads), 0)
                col = lax.broadcasted_iota(jnp.int32, (PAD, z.heads), 1)
                group = lax.rem(me + k, n)
                pick = jnp.where((row < z.local) & (col == row + group * z.local), 1.0, 0.0).astype(BF16)
                wide = jnp.concatenate(
                    [dot(pick, ld_ref[...], (1, 0)), jnp.zeros((PAD, LANES - rows), F32)], axis=1
                )
                outs[i][height - PAD : height, :] = wide.astype(BF16)

    args = [lengths, *(pltpu.with_memory_space_constraint(a, pltpu.HBM) for a in (low_rank, *bases, edit_up))]
    specs = [SMEM, *([pl.BlockSpec(memory_space=pltpu.HBM)] * (kinds + 2))]
    if decays:
        args.append(log_decay)
        specs.append(pl.BlockSpec(memory_space=pltpu.VMEM))
    scratch = [
        pltpu.VMEM((n * kinds, rows, count * dh), BF16),
        pltpu.VMEM((n * kinds, rank, count * dh), BF16),
        pltpu.VMEM(low_rank.shape, BF16),
        pltpu.SemaphoreType.DMA((2, n * kinds + 1)),
    ]
    shapes = [((n, height, dh), BF16)] if whole else [((height, dh), BF16)] * len(places)
    return call(kernel, shapes, args, specs, scratch, after)


def scatter_heads(z, refs, held, first, count):
    me = lax.axis_index("inner")
    for k in range(z.n):
        chunk = lax.rem(me + (z.n - k), z.n)
        at = pl.ds(pl.multiple_of(chunk * z.rows, z.rows), z.rows)
        for h in range(count):
            top = (first + h) * z.rows
            held[h, at, :] = refs[k][top : top + z.rows, :]


def segment_states(z, part, kv, decays=None, after=()):
    h0, count = part
    n, rows, dh, seg = z.n, z.rows, z.dh, z.seg
    first = decays is None

    def kernel(*refs):
        kv_refs, refs = refs[:n], refs[n:]
        if first:
            state, send, col_ref, row_ref, ks, vs, lds = refs
        else:
            col_ref, row_ref, state, send, ks, vs = refs
        if first:
            me = lax.axis_index("inner")
            for k in range(n):
                lds[lax.rem(me + (n - k), n)] = kv_refs[k][2 * z.local * rows :, :]
            t = lax.broadcasted_iota(jnp.int32, (rows, LANES), 0)
            s = lax.broadcasted_iota(jnp.int32, (rows, LANES), 1)
            tri = jnp.where(s <= t, 1.0, 0.0).astype(BF16)
            so_far = jnp.zeros((1, PAD), F32)
            for j in range(n):
                cum = dot(tri, lds[j], (1, 1)) + so_far
                so_far = cum[rows - 1 : rows, :]
                wide = jnp.concatenate([cum, jnp.zeros((rows, LANES - PAD), F32)], axis=1)
                col_ref[j * rows : (j + 1) * rows, :] = wide
            row_ref[...] = col_ref[...].T[:PAD, :]
        scatter_heads(z, kv_refs, ks, h0, count)
        scatter_heads(z, kv_refs, vs, z.local + h0, count)
        col = col_ref[...]
        scale = jnp.exp(col[seg - 1 : seg, :] - col)
        for h in range(count):
            scaled = (ks[h].astype(F32) * scale[:, h0 + h : h0 + h + 1]).astype(BF16)
            value = dot(scaled, vs[h], (0, 0))
            state[h * dh : (h + 1) * dh, :] = value
            send[h * dh : (h + 1) * dh, :] = value.astype(BF16)
        put_sums(send, count * dh, jnp.broadcast_to(row_ref[:, seg - 1 : seg], (PAD, LANES)))

    shapes = [((count * dh, dh), F32), ((count * dh + 2 * PAD, dh), BF16)]
    scratch = [pltpu.VMEM((count, seg, dh), BF16)] * 2
    if first:
        shapes += [((seg, LANES), F32), ((PAD, seg), F32)]
        scratch.append(pltpu.VMEM((n, PAD, LANES), BF16))
    return call(kernel, shapes, [*kv, *(decays or ())], scratch=scratch, after=after)


def put_sums(send, at, sums):
    high = sums.astype(BF16)
    send[at : at + PAD, :] = high
    send[at + PAD : at + 2 * PAD, :] = (sums - high.astype(F32)).astype(BF16)


def get_sums(got, at):
    return got[at : at + PAD, :].astype(F32) + got[at + PAD : at + 2 * PAD, :].astype(F32)


def digit_of(step):
    shift, width = step
    return lax.rem(lax.axis_index("ctx") // (1 << shift), 1 << width)


def exchange(step, send):
    shift, width = step
    size = lax.axis_size("ctx")
    return [
        lax.ppermute(send, "ctx", [(i, i ^ (m << shift)) for i in range(size)]) for m in range(1, 1 << width)
    ]


def weights_of(step, others):
    mine = digit_of(step)
    at = [mine ^ (m + 1) for m in range(len(others))]
    zero = jnp.zeros_like(others[0])
    before = []
    for a in at:
        between = zero
        for b, other in zip(at, others):
            between = between + jnp.where((a < b) & (b < mine), other, 0.0)
        before.append(jnp.where(a < mine, jnp.exp(between), 0.0))
    return mine, at, before


def join(z, step, part, total, got, sums, carried=None, final=False):
    h0, count = part
    dh, parts = z.dh, len(got)

    def kernel(*refs):
        total_ref, sums_ref = refs[:2]
        got_refs = refs[2 : 2 + parts]
        carried_ref = refs[2 + parts] if carried is not None else None
        new_carried, send, new_sums = refs[-3:]
        new_total = None if final else refs[-4]
        if carried is None:
            own = jnp.broadcast_to(sums_ref[:, z.seg - 1 : z.seg], (PAD, LANES))
            ahead = jnp.zeros((PAD, LANES), F32)
        else:
            own, ahead = sums_ref[:PAD, :], sums_ref[PAD:, :]
        others = [get_sums(ref, count * dh) for ref in got_refs]
        mine, at, before = weights_of(step, others)
        whole, passed = own, jnp.zeros((PAD, LANES), F32)
        keep = jnp.zeros((PAD, LANES), F32)
        takes = []
        for a, other in zip(at, others):
            whole = whole + other
            passed = passed + jnp.where(a < mine, other, 0.0)
            keep = keep + jnp.where(a > mine, other, 0.0)
            behind = jnp.where(mine > a, own, 0.0)
            for b, third in zip(at, others):
                behind = behind + jnp.where(b > a, third, 0.0)
            takes.append(jnp.exp(behind))
        keep, lead = jnp.exp(keep), jnp.exp(ahead)
        for h in range(count):
            rows = slice(h * dh, (h + 1) * dh)
            row = slice(h0 + h, h0 + h + 1)
            value = total_ref[rows, :] * keep[row, :]
            moved = jnp.zeros((dh, dh), F32)
            for ref, take, weight in zip(got_refs, takes, before):
                theirs = ref[rows, :].astype(F32)
                value = value + theirs * take[row, :]
                moved = moved + theirs * (weight * lead)[row, :]
            if not final:
                new_total[rows, :] = value
            send[rows, :] = value.astype(BF16)
            new_carried[rows, :] = moved if carried is None else carried_ref[rows, :] + moved
        put_sums(send, count * dh, whole)
        new_sums[:PAD, :] = whole
        new_sums[PAD:, :] = ahead + passed

    shapes = [((count * dh, dh), F32)] * (1 if final else 2)
    shapes += [((count * dh + 2 * PAD, dh), BF16), ((2 * PAD, LANES), F32)]
    args = [total, sums, *got] + ([] if carried is None else [carried])
    return call(kernel, shapes, args)


def attend(z, part, kv, qs_in, col, row, carried, got, sums):
    h0, count = part
    n, rows, dh, seg = z.n, z.rows, z.dh, z.seg

    def kernel(*refs):
        kv_refs, q_refs = refs[:n], refs[n : n + 1]
        col_ref, row_ref, carried_ref, sums_ref = refs[n + 1 : n + 5]
        got_refs = refs[n + 5 : n + 5 + len(got)]
        outs = refs[-n - 4 : -4]
        ks, vs, qs, mixed = refs[-4:]
        scatter_heads(z, kv_refs, ks, h0, count)
        scatter_heads(z, kv_refs, vs, z.local + h0, count)
        for chunk in range(n):
            for h in range(count):
                rows_of = slice((h0 + h) * rows, (h0 + h + 1) * rows)
                qs[h, chunk * rows : (chunk + 1) * rows, :] = q_refs[0][chunk, rows_of, :]
        before = weights_of(z.steps[-1], [get_sums(ref, count * dh) for ref in got_refs])[2]
        lead = jnp.exp(sums_ref[PAD:, :])
        before = [weight * lead for weight in before]
        t = lax.broadcasted_iota(jnp.int32, (seg, seg), 0)
        s = lax.broadcasted_iota(jnp.int32, (seg, seg), 1)
        causal = s <= t
        for h in range(count):
            at = slice(h * dh, (h + 1) * dh)
            former = carried_ref[at, :]
            for ref, weight in zip(got_refs, before):
                former = former + ref[at, :].astype(F32) * weight[h0 + h : h0 + h + 1, :]
            q = qs[h]
            d_col = col_ref[:, h0 + h : h0 + h + 1]
            scores = dot(q, ks[h], (1, 1))
            gap = jnp.where(causal, d_col - row_ref[h0 + h : h0 + h + 1, :], 0.0)
            weights = jnp.where(causal, scores * jnp.exp(gap), 0.0).astype(BF16)
            out = dot(weights, vs[h], (1, 0)) + jnp.exp(d_col) * dot(q, former.astype(BF16), (1, 0))
            mixed[:, at] = out.astype(BF16)
        me = lax.axis_index("inner")
        for k in range(n):
            chunk = lax.rem(me + k, n)
            outs[k][...] = mixed[pl.ds(pl.multiple_of(chunk * rows, rows), rows), :]

    scratch = [pltpu.VMEM((count, seg, dh), BF16)] * 3 + [pltpu.VMEM((seg, count * dh), BF16)]
    args = [*kv, *qs_in, col, row, carried, sums, *got]
    return call(kernel, [((rows, count * dh), BF16)] * n, args, scratch=scratch)


def lane_squares(total, refs):
    for ref in refs:
        for at in range(0, ref.shape[1], LANES):
            flat = ref[:, at : at + LANES].astype(F32)
            total = total + flat * flat
    return total


def squares(z, blocks):
    def kernel(*refs):
        refs[-1][...] = lane_squares(jnp.zeros((z.rows, LANES), F32), refs[:-1])

    return call(kernel, [((z.rows, LANES), F32)], blocks)[0]


def normalize(z, lengths, gain, blocks):
    n, rows, dh = z.n, z.rows, z.dh
    early = squares(z, [block for part in blocks[:-1] for block in part])

    def kernel(len_ref, gain_ref, early_ref, *refs):
        *refs, far, out, sems = refs
        me = lax.axis_index("inner")
        live = live_mask(len_ref, rows)
        total = jnp.sum(lane_squares(early_ref[...], refs[-n:]), axis=1, keepdims=True)
        inv = lax.rsqrt(total / z.width + 1e-06)
        copies = []
        for k in range(n):
            first = lax.rem(me + (n - k), n) * z.local
            for p, (h0, count) in enumerate(z.parts):
                cols = pl.ds(pl.multiple_of((first + h0) * dh, LANES), count * dh)
                scaled = refs[p * n + k][...].astype(F32) * inv * gain_ref[:, cols]
                out[:, cols] = jnp.where(live, scaled, 0.0).astype(BF16)
            cols = pl.ds(pl.multiple_of(first * dh, LANES), z.local * dh)
            copies.append(pltpu.make_async_copy(out.at[:, cols], far.at[:, cols], sems.at[k]))
            copies[-1].start()
        for copy in copies:
            copy.wait()

    args = [lengths, gain, early, *(block for part in blocks for block in part)]
    specs = [SMEM] + [pl.BlockSpec(memory_space=pltpu.VMEM)] * (len(args) - 1)
    scratch = [pltpu.VMEM((rows, z.width), BF16), pltpu.SemaphoreType.DMA((n,))]
    return call(kernel, [((rows, z.width), BF16)], args, specs, scratch, out=pltpu.HBM)[0]


def shift_blocks(z, blocks):
    n = z.n
    return [blocks[0]] + [
        lax.ppermute(blocks[k], "inner", [(i, (i + k) % n) for i in range(n)]) for k in range(1, n)
    ]


def shards(low_rank, q_base, k_base, v_base, edit_up, log_decay, lengths, norm_gain):
    z = Sizes(q_base, log_decay)
    every = (0, z.local)
    low_rank, log_decay = low_rank.T, log_decay.T
    kv = [None] * z.n
    first = z.n // 2
    for ks in ((first,), tuple(k for k in range(1, z.n) if k != first) + (0,)):
        made = project(
            z, "kv", every, lengths, low_rank, (k_base, v_base), edit_up, (1, 2), log_decay, True, places=ks
        )
        for k, block in zip(ks, made):
            kv[k] = block
    kv = shift_blocks(z, kv)
    qs = project(z, "q", every, lengths, low_rank, (q_base,), edit_up, (0,), log_decay, False, whole=True)
    qs = gate(qs, (kv[first],))
    qs = [lax.all_to_all(qs[0], "inner", split_axis=0, concat_axis=0, tiled=True)]
    outs = []
    decays = None
    for p, part in enumerate(z.parts):
        total, send, *made = segment_states(z, part, kv, decays)
        decays = decays or made
        carried, sums = None, decays[1]
        for step in z.steps[:-1]:
            final = step is z.steps[-2]
            got = exchange(step, send)
            *total, carried, send, sums = join(z, step, part, total, got, sums, carried, final)
            total = total[0] if total else None
        got = exchange(z.steps[-1], send)
        outs.append(shift_blocks(z, attend(z, part, kv, qs, *decays, carried, got, sums)))
    return normalize(z, lengths, norm_gain[None, :], outs)


def solution(mesh):
    rows = P(("ctx", "inner"), None)
    return jax.shard_map(
        shards,
        mesh=mesh,
        in_specs=(rows, rows, rows, rows, P(), rows, P("ctx"), P()),
        out_specs=rows,
        check_vma=False,
    )
```

```python
import jax
import jax.numpy as jnp
from jax import lax
from jax.experimental import pallas as pl
from jax.experimental.pallas import tpu as pltpu
from jax.sharding import PartitionSpec as P

F32, BF16 = jnp.float32, jnp.bfloat16
LANES = 128
PAD = 16
PARTS = 2
PARAMS = pltpu.CompilerParams(vmem_limit_bytes=32 * 1024 * 1024)
COST = pl.CostEstimate(flops=1000000000, bytes_accessed=1, transcendentals=0)
SMEM = pl.BlockSpec(memory_space=pltpu.SMEM)


def dot(a, b, dims):
    return lax.dot_general(a, b, ((dims[:1], dims[1:]), ((), ())), preferred_element_type=F32)


def call(kernel, shapes, args, specs=None, scratch=(), after=(), out=pltpu.VMEM):
    whole = [pl.BlockSpec(memory_space=pltpu.VMEM)] * len(args) if specs is None else specs
    if after:
        inner, used = kernel, len(args)

        def kernel(*refs):
            inner(*refs[:used], *refs[used + len(after) :])

        args = [*args, *after]
        whole = [*whole, *([pl.BlockSpec(memory_space=pl.ANY)] * len(after))]
    return pl.pallas_call(
        kernel,
        out_shape=[jax.ShapeDtypeStruct(*shape) for shape in shapes],
        in_specs=whole,
        out_specs=[pl.BlockSpec(memory_space=out)] * len(shapes),
        scratch_shapes=list(scratch),
        compiler_params=PARAMS,
        cost_estimate=COST,
    )(*args)


def gate(arrays, after):
    every = pl.BlockSpec(memory_space=pl.ANY)
    return pl.pallas_call(
        lambda *refs: None,
        out_shape=[jax.ShapeDtypeStruct(a.shape, a.dtype) for a in arrays],
        in_specs=[every] * (len(arrays) + len(after)),
        out_specs=[every] * len(arrays),
        input_output_aliases={i: i for i in range(len(arrays))},
        compiler_params=PARAMS,
    )(*arrays, *after)


def live_mask(len_ref, rows):
    at = lax.axis_index("inner") * rows + lax.broadcasted_iota(jnp.int32, (rows, 1), 0)
    return at < len_ref[0]


class Sizes:
    def __init__(self, q_base, log_decay):
        self.n = lax.axis_size("inner")
        self.rows, self.width = q_base.shape
        self.heads = log_decay.shape[1]
        self.local = self.heads // self.n
        self.dh = self.width // self.heads
        self.seg = self.rows * self.n
        bits = (lax.axis_size("ctx") - 1).bit_length()
        self.steps = [(at, 1) for at in range(bits)]
        first = max(1, self.local // PARTS)
        self.parts = [(at, min(first, self.local - at)) for at in range(0, first * PARTS, first) if at < self.local]
        self.parts[-1] = (self.parts[-1][0], self.local - self.parts[-1][0])


def project(z, names, part, lengths, low_rank, bases, edit_up, columns, log_decay, decays, after=(), whole=False, places=None):
    h0, count = part
    n, rows, dh = z.n, z.rows, z.dh
    kinds = len(bases)
    rank = edit_up.shape[0]
    places = places or (*range(1, n), 0)
    height = kinds * count * rows + (PAD if decays else 0)

    def kernel(len_ref, lr_ref, *refs):
        base_refs, up_ref = refs[:kinds], refs[kinds]
        ld_ref = refs[kinds + 1] if decays else None
        me = lax.axis_index("inner")
        if whole:
            outs = [refs[-5].at[lax.rem(me + k, n)] for k in places]
        else:
            outs = refs[-len(places) - 4 : -4]
        base_buf, up_buf, low_buf, sems = refs[-4:]

        def copies(i):
            at = (lax.rem(me + places[i], n) * z.local + h0) * dh
            for kind in range(kinds):
                cols = pl.ds(pl.multiple_of(at, LANES), count * dh)
                up_cols = pl.ds(pl.multiple_of(at + columns[kind] * z.width, LANES), count * dh)
                slot = i * kinds + kind
                yield pltpu.make_async_copy(base_refs[kind].at[:, cols], base_buf.at[slot], sems.at[0, slot])
                yield pltpu.make_async_copy(up_ref.at[:, up_cols], up_buf.at[slot], sems.at[1, slot])

        small = pltpu.make_async_copy(lr_ref, low_buf, sems.at[0, n * kinds])
        small.start()
        for i in range(len(places)):
            for copy in copies(i):
                copy.start()
        live = live_mask(len_ref, rows)
        small.wait()
        low = low_buf[...].T
        for i, k in enumerate(places):
            for copy in copies(i):
                copy.wait()
            for kind in range(kinds):
                slot = i * kinds + kind
                edited = base_buf[slot].astype(F32) + dot(low, up_buf[slot], (1, 0))
                if names[kind] != "q":
                    edited = jnp.where(live, edited, 0.0)
                edited = edited.astype(BF16)
                for h in range(count):
                    top = (kind * count + h) * rows
                    outs[i][top : top + rows, :] = edited[:, h * dh : (h + 1) * dh]
            if decays:
                row = lax.broadcasted_iota(jnp.int32, (PAD, z.heads), 0)
                col = lax.broadcasted_iota(jnp.int32, (PAD, z.heads), 1)
                group = lax.rem(me + k, n)
                pick = jnp.where((row < z.local) & (col == row + group * z.local), 1.0, 0.0).astype(BF16)
                wide = jnp.concatenate(
                    [dot(pick, ld_ref[...], (1, 0)), jnp.zeros((PAD, LANES - rows), F32)], axis=1
                )
                outs[i][height - PAD : height, :] = wide.astype(BF16)

    args = [lengths, *(pltpu.with_memory_space_constraint(a, pltpu.HBM) for a in (low_rank, *bases, edit_up))]
    specs = [SMEM, *([pl.BlockSpec(memory_space=pltpu.HBM)] * (kinds + 2))]
    if decays:
        args.append(log_decay)
        specs.append(pl.BlockSpec(memory_space=pltpu.VMEM))
    scratch = [
        pltpu.VMEM((n * kinds, rows, count * dh), BF16),
        pltpu.VMEM((n * kinds, rank, count * dh), BF16),
        pltpu.VMEM(low_rank.shape, BF16),
        pltpu.SemaphoreType.DMA((2, n * kinds + 1)),
    ]
    shapes = [((n, height, dh), BF16)] if whole else [((height, dh), BF16)] * len(places)
    return call(kernel, shapes, args, specs, scratch, after)


def scatter_heads(z, refs, held, first, count):
    me = lax.axis_index("inner")
    for k in range(z.n):
        chunk = lax.rem(me + (z.n - k), z.n)
        at = pl.ds(pl.multiple_of(chunk * z.rows, z.rows), z.rows)
        for h in range(count):
            top = (first + h) * z.rows
            held[h, at, :] = refs[k][top : top + z.rows, :]


def segment_states(z, part, kv, decays=None, after=()):
    h0, count = part
    n, rows, dh, seg = z.n, z.rows, z.dh, z.seg
    first = decays is None

    def kernel(*refs):
        kv_refs, refs = refs[:n], refs[n:]
        if first:
            state, send, col_ref, row_ref, ks, vs, lds = refs
        else:
            col_ref, row_ref, state, send, ks, vs = refs
        if first:
            me = lax.axis_index("inner")
            for k in range(n):
                lds[lax.rem(me + (n - k), n)] = kv_refs[k][2 * z.local * rows :, :]
            t = lax.broadcasted_iota(jnp.int32, (rows, LANES), 0)
            s = lax.broadcasted_iota(jnp.int32, (rows, LANES), 1)
            tri = jnp.where(s <= t, 1.0, 0.0).astype(BF16)
            so_far = jnp.zeros((1, PAD), F32)
            for j in range(n):
                cum = dot(tri, lds[j], (1, 1)) + so_far
                so_far = cum[rows - 1 : rows, :]
                wide = jnp.concatenate([cum, jnp.zeros((rows, LANES - PAD), F32)], axis=1)
                col_ref[j * rows : (j + 1) * rows, :] = wide
            row_ref[...] = col_ref[...].T[:PAD, :]
        scatter_heads(z, kv_refs, ks, h0, count)
        scatter_heads(z, kv_refs, vs, z.local + h0, count)
        col = col_ref[...]
        scale = jnp.exp(col[seg - 1 : seg, :] - col)
        scaled = [
            (ks[h].astype(F32) * scale[:, h0 + h : h0 + h + 1]).astype(BF16) for h in range(count)
        ]
        values = [dot(scaled[h], vs[h], (0, 0)) for h in range(count)]
        for h, value in enumerate(values):
            state[h * dh : (h + 1) * dh, :] = value
            send[h * dh : (h + 1) * dh, :] = value.astype(BF16)
        put_sums(send, count * dh, jnp.broadcast_to(row_ref[:, seg - 1 : seg], (PAD, LANES)))

    shapes = [((count * dh, dh), F32), ((count * dh + 2 * PAD, dh), BF16)]
    scratch = [pltpu.VMEM((count, seg, dh), BF16)] * 2
    if first:
        shapes += [((seg, LANES), F32), ((PAD, seg), F32)]
        scratch.append(pltpu.VMEM((n, PAD, LANES), BF16))
    return call(kernel, shapes, [*kv, *(decays or ())], scratch=scratch, after=after)


def put_sums(send, at, sums):
    high = sums.astype(BF16)
    send[at : at + PAD, :] = high
    send[at + PAD : at + 2 * PAD, :] = (sums - high.astype(F32)).astype(BF16)


def get_sums(got, at):
    return got[at : at + PAD, :].astype(F32) + got[at + PAD : at + 2 * PAD, :].astype(F32)


def digit_of(step):
    shift, width = step
    return lax.rem(lax.axis_index("ctx") // (1 << shift), 1 << width)


def exchange(step, send):
    shift, width = step
    size = lax.axis_size("ctx")
    return [
        lax.ppermute(send, "ctx", [(i, i ^ (m << shift)) for i in range(size)]) for m in range(1, 1 << width)
    ]


def weights_of(step, others):
    mine = digit_of(step)
    at = [mine ^ (m + 1) for m in range(len(others))]
    zero = jnp.zeros_like(others[0])
    before = []
    for a in at:
        between = zero
        for b, other in zip(at, others):
            between = between + jnp.where((a < b) & (b < mine), other, 0.0)
        before.append(jnp.where(a < mine, jnp.exp(between), 0.0))
    return mine, at, before


def join(z, step, part, total, got, sums, carried=None, final=False):
    h0, count = part
    dh, parts = z.dh, len(got)

    def kernel(*refs):
        total_ref, sums_ref = refs[:2]
        got_refs = refs[2 : 2 + parts]
        carried_ref = refs[2 + parts] if carried is not None else None
        new_carried, send, new_sums = refs[-3:]
        new_total = None if final else refs[-4]
        if carried is None:
            own = jnp.broadcast_to(sums_ref[:, z.seg - 1 : z.seg], (PAD, LANES))
            ahead = jnp.zeros((PAD, LANES), F32)
        else:
            own, ahead = sums_ref[:PAD, :], sums_ref[PAD:, :]
        others = [get_sums(ref, count * dh) for ref in got_refs]
        mine, at, before = weights_of(step, others)
        whole, passed = own, jnp.zeros((PAD, LANES), F32)
        keep = jnp.zeros((PAD, LANES), F32)
        takes = []
        for a, other in zip(at, others):
            whole = whole + other
            passed = passed + jnp.where(a < mine, other, 0.0)
            keep = keep + jnp.where(a > mine, other, 0.0)
            behind = jnp.where(mine > a, own, 0.0)
            for b, third in zip(at, others):
                behind = behind + jnp.where(b > a, third, 0.0)
            takes.append(jnp.exp(behind))
        keep, lead = jnp.exp(keep), jnp.exp(ahead)
        for h in range(count):
            rows = slice(h * dh, (h + 1) * dh)
            row = slice(h0 + h, h0 + h + 1)
            value = total_ref[rows, :] * keep[row, :]
            moved = jnp.zeros((dh, dh), F32)
            for ref, take, weight in zip(got_refs, takes, before):
                theirs = ref[rows, :].astype(F32)
                value = value + theirs * take[row, :]
                moved = moved + theirs * (weight * lead)[row, :]
            if not final:
                new_total[rows, :] = value
            send[rows, :] = value.astype(BF16)
            new_carried[rows, :] = moved if carried is None else carried_ref[rows, :] + moved
        put_sums(send, count * dh, whole)
        new_sums[:PAD, :] = whole
        new_sums[PAD:, :] = ahead + passed

    shapes = [((count * dh, dh), F32)] * (1 if final else 2)
    shapes += [((count * dh + 2 * PAD, dh), BF16), ((2 * PAD, LANES), F32)]
    args = [total, sums, *got] + ([] if carried is None else [carried])
    return call(kernel, shapes, args)


def attend(z, part, kv, qs_in, col, row, carried, got, sums):
    h0, count = part
    n, rows, dh, seg = z.n, z.rows, z.dh, z.seg

    def kernel(*refs):
        kv_refs, q_refs = refs[:n], refs[n : n + 1]
        col_ref, row_ref, carried_ref, sums_ref = refs[n + 1 : n + 5]
        got_refs = refs[n + 5 : n + 5 + len(got)]
        outs = refs[-n - 4 : -4]
        ks, vs, qs, mixed = refs[-4:]
        scatter_heads(z, kv_refs, ks, h0, count)
        scatter_heads(z, kv_refs, vs, z.local + h0, count)
        for chunk in range(n):
            for h in range(count):
                rows_of = slice((h0 + h) * rows, (h0 + h + 1) * rows)
                qs[h, chunk * rows : (chunk + 1) * rows, :] = q_refs[0][chunk, rows_of, :]
        before = weights_of(z.steps[-1], [get_sums(ref, count * dh) for ref in got_refs])[2]
        lead = jnp.exp(sums_ref[PAD:, :])
        before = [weight * lead for weight in before]
        t = lax.broadcasted_iota(jnp.int32, (seg, seg), 0)
        s = lax.broadcasted_iota(jnp.int32, (seg, seg), 1)
        causal = s <= t
        scores = [dot(qs[h], ks[h], (1, 1)) for h in range(count)]
        inter = []
        for h in range(count):
            at = slice(h * dh, (h + 1) * dh)
            former = carried_ref[at, :]
            for ref, weight in zip(got_refs, before):
                former = former + ref[at, :].astype(F32) * weight[h0 + h : h0 + h + 1, :]
            inter.append(dot(qs[h], former.astype(BF16), (1, 0)))
        weights = []
        for h in range(count):
            gap = jnp.where(causal, col_ref[:, h0 + h : h0 + h + 1] - row_ref[h0 + h : h0 + h + 1, :], 0.0)
            weights.append(jnp.where(causal, scores[h] * jnp.exp(gap), 0.0).astype(BF16))
        totals = [dot(weights[h], vs[h], (1, 0)) for h in range(count)]
        for h in range(count):
            out = totals[h] + jnp.exp(col_ref[:, h0 + h : h0 + h + 1]) * inter[h]
            mixed[:, h * dh : (h + 1) * dh] = out.astype(BF16)
        me = lax.axis_index("inner")
        for k in range(n):
            chunk = lax.rem(me + k, n)
            outs[k][...] = mixed[pl.ds(pl.multiple_of(chunk * rows, rows), rows), :]

    scratch = [pltpu.VMEM((count, seg, dh), BF16)] * 3 + [pltpu.VMEM((seg, count * dh), BF16)]
    args = [*kv, *qs_in, col, row, carried, sums, *got]
    return call(kernel, [((rows, count * dh), BF16)] * n, args, scratch=scratch)


def lane_squares(total, refs):
    for ref in refs:
        for at in range(0, ref.shape[1], LANES):
            flat = ref[:, at : at + LANES].astype(F32)
            total = total + flat * flat
    return total


def squares(z, blocks):
    def kernel(*refs):
        refs[-1][...] = lane_squares(jnp.zeros((z.rows, LANES), F32), refs[:-1])

    return call(kernel, [((z.rows, LANES), F32)], blocks)[0]


def normalize(z, lengths, gain, blocks):
    n, rows, dh = z.n, z.rows, z.dh
    early = squares(z, [block for part in blocks[:-1] for block in part])

    def kernel(len_ref, gain_ref, early_ref, *refs):
        *refs, far, out, sems = refs
        me = lax.axis_index("inner")
        live = live_mask(len_ref, rows)
        total = jnp.sum(lane_squares(early_ref[...], refs[-n:]), axis=1, keepdims=True)
        inv = lax.rsqrt(total / z.width + 1e-06)
        copies = []
        for k in range(n):
            first = lax.rem(me + (n - k), n) * z.local
            for p, (h0, count) in enumerate(z.parts):
                cols = pl.ds(pl.multiple_of((first + h0) * dh, LANES), count * dh)
                scaled = refs[p * n + k][...].astype(F32) * inv * gain_ref[:, cols]
                out[:, cols] = jnp.where(live, scaled, 0.0).astype(BF16)
            cols = pl.ds(pl.multiple_of(first * dh, LANES), z.local * dh)
            copies.append(pltpu.make_async_copy(out.at[:, cols], far.at[:, cols], sems.at[k]))
            copies[-1].start()
        for copy in copies:
            copy.wait()

    args = [lengths, gain, early, *(block for part in blocks for block in part)]
    specs = [SMEM] + [pl.BlockSpec(memory_space=pltpu.VMEM)] * (len(args) - 1)
    scratch = [pltpu.VMEM((rows, z.width), BF16), pltpu.SemaphoreType.DMA((n,))]
    return call(kernel, [((rows, z.width), BF16)], args, specs, scratch, out=pltpu.HBM)[0]


def shift_blocks(z, blocks):
    n = z.n
    return [blocks[0]] + [
        lax.ppermute(blocks[k], "inner", [(i, (i + k) % n) for i in range(n)]) for k in range(1, n)
    ]


def shards(low_rank, q_base, k_base, v_base, edit_up, log_decay, lengths, norm_gain):
    z = Sizes(q_base, log_decay)
    every = (0, z.local)
    low_rank, log_decay = low_rank.T, log_decay.T
    kv = [None] * z.n
    first = z.n // 2
    for ks in ((first,), tuple(k for k in range(1, z.n) if k != first) + (0,)):
        made = project(
            z, "kv", every, lengths, low_rank, (k_base, v_base), edit_up, (1, 2), log_decay, True, places=ks
        )
        for k, block in zip(ks, made):
            kv[k] = block
    kv = shift_blocks(z, kv)
    qs = project(z, "q", every, lengths, low_rank, (q_base,), edit_up, (0,), log_decay, False, whole=True)
    qs = gate(qs, (kv[first],))
    qs = [lax.all_to_all(qs[0], "inner", split_axis=0, concat_axis=0, tiled=True)]
    outs = []
    decays = None
    for p, part in enumerate(z.parts):
        total, send, *made = segment_states(z, part, kv, decays)
        decays = decays or made
        carried, sums = None, decays[1]
        for step in z.steps[:-1]:
            final = step is z.steps[-2]
            got = exchange(step, send)
            *total, carried, send, sums = join(z, step, part, total, got, sums, carried, final)
            total = total[0] if total else None
        got = exchange(z.steps[-1], send)
        outs.append(shift_blocks(z, attend(z, part, kv, qs, *decays, carried, got, sums)))
    return normalize(z, lengths, norm_gain[None, :], outs)


def solution(mesh):
    rows = P(("ctx", "inner"), None)
    return jax.shard_map(
        shards,
        mesh=mesh,
        in_specs=(rows, rows, rows, rows, P(), rows, P("ctx"), P()),
        out_specs=rows,
        check_vma=False,
    )
```
